128 devices in a mesh: tenant: 8 (over x, core), fsdp: 16 (over y, z).
Axes of the slice: x: 4, y: 4, z: 4, core: 2. Of those that a mesh axis runs over, the one named last changes fastest.
Arguments:
- tokens: bfloat16 [65536, 8192], P(('tenant', 'fsdp')), may hold values from -6 to 6
- cotangent: bfloat16 [65536, 1024], P(('tenant', 'fsdp')), may hold values from -6 to 6
- value_weight: bfloat16 [8192, 1024], P('fsdp'), may hold values from -0.0625 to 0.0625
- adapters: float32 [128, 16, 9216], P('tenant', None, 'fsdp'), may hold values from -2.5 to 2.5
- first_moment: float32 [128, 16, 9216], P('tenant', None, 'fsdp'), may hold values from -4 to 4
- second_moment: float32 [128, 16, 9216], P('tenant', None, 'fsdp'), may hold values from 0.2 to 2
- tenant_home: int32 [128], replicated, may hold values from 0 to 127, as said below
- read_tenants: int32 [128, 8], replicated, may hold values from 0 to 127, as said below
- row_tenant: int32 [65536], P(('tenant', 'fsdp')), may hold values from 0 to 127, as said below
Outputs:
- values: bfloat16 [65536, 1024], P(('tenant', 'fsdp'))
- token_grad: bfloat16 [65536, 8192], P(('tenant', 'fsdp'))
- new_adapters: float32 [128, 16, 9216], P('tenant', None, 'fsdp')
- new_first: float32 [128, 16, 9216], P('tenant', None, 'fsdp')
- new_second: float32 [128, 16, 9216], P('tenant', None, 'fsdp')
- refreshed: bfloat16 [1024, 16, 9216], P(('tenant', 'fsdp'))
The draws below stay inside these ranges and needn't reach their ends.
Inputs may be any that keep to these rules, and one draw needn't show every extreme that they name: `tenant_home`: a permutation: every slot holds exactly one tenant; slot h belongs to index h // 16 of tenant. `read_tenants`: in each row, entry k is a tenant whose slot lies in index k of tenant. `row_tenant`: every row's tenant is in the read list of its block, and every entry of a block's read list is the tenant of some row of that block.
All inputs are finite; a program needn't handle non-finite values.
Results may differ from the reference program's by a relative error of at most 0.0055.
Values may be sent and summed in bfloat16 or wider, within the bound.
No kernel may reach another device: no remote copies, remote signals or barrier semaphores. Data moves between devices by JAX's collectives and lax.ppermute only.
A program may use at most 128 MiB of HBM per device.

```python
import math
import jax
import jax.numpy as jnp
from jax import lax

MODEL_WIDTH = 8192
KV = 1024
ADAPTER_RANK = 16
TOK_DEV = 512
SLOTS = 16
PER_OWNER = 1
W_AD = 9216
TENANTS = 128
READS = 8
ROWS = 65536
N_TENANT = 8
N_FSDP = 16


def layout(key):
    perm_key = jax.random.fold_in(key, 11)
    pick_key = jax.random.fold_in(key, 12)
    row_key = jax.random.fold_in(key, 13)
    device_count = N_TENANT * N_FSDP
    home_of = jax.random.permutation(perm_key, TENANTS).astype(jnp.int32)
    tenant_at = jnp.argsort(home_of, stable=True).astype(jnp.int32)
    pick_keys = jax.random.split(pick_key, device_count * N_TENANT)
    picks = jax.vmap(lambda sub_key: jax.random.permutation(sub_key, SLOTS)[:PER_OWNER])(pick_keys).astype(jnp.int32)
    owners = (jnp.arange(device_count * N_TENANT) % N_TENANT).astype(jnp.int32)
    home_pick = owners[:, None] * SLOTS + picks
    read_list = jnp.take(tenant_at, home_pick.reshape(-1), axis=0).reshape(device_count, READS).astype(jnp.int32)
    row_pick = jax.random.randint(row_key, (device_count, TOK_DEV), 0, READS).astype(jnp.int32)
    row_pick = row_pick.at[:, :READS].set(jnp.arange(READS, dtype=jnp.int32)[None, :])
    row_list = jnp.take_along_axis(read_list, row_pick, axis=1).reshape(-1).astype(jnp.int32)
    return (home_of, read_list, row_list)


def draw_tenant_home(key, part):
    return layout(key)[0]


def draw_read_tenants(key, part):
    return layout(key)[1]


def draw_row_tenant(key, part):
    return layout(key)[2]


def block_scale(key, shape, cuts, least, largest):
    def one(dim, shards_of):
        draws = jax.random.uniform(jax.random.fold_in(jax.random.fold_in(key, 6), dim), (shards_of,), jnp.float32, least / len(cuts), largest / len(cuts))
        return jnp.repeat(jnp.exp(draws), shape[dim] // shards_of).reshape((-1,) + (1,) * (len(shape) - dim - 1))

    loudness = one(*cuts[0])
    for cut in cuts[1:]:
        loudness = loudness * one(*cut)
    return loudness


def gaussian(rng, dims, spread, bound, cuts=(), kind=jnp.bfloat16):
    factor_of = block_scale(rng, dims, cuts, -0.22, 0.18) if cuts else 1.0
    result = jax.random.normal(rng, dims, jnp.float32) * spread * factor_of
    return jnp.minimum(jnp.maximum(result, -bound), bound).astype(kind)


def setup_inputs(seed: int = 0) -> dict:
    key_of = jax.random.split(jax.random.key(seed), 10)
    return {
        "tokens": gaussian(key_of[0], (ROWS, MODEL_WIDTH), 1.0, 6.0, ((0, 128),)),
        "cotangent": gaussian(key_of[1], (ROWS, KV), 1.0, 6.0, ((0, 128),)),
        "value_weight": gaussian(key_of[2], (MODEL_WIDTH, KV), MODEL_WIDTH ** -0.5, 0.0625, ((0, 16),)),
        "adapters": gaussian(key_of[3], (TENANTS, ADAPTER_RANK, W_AD), 0.5, 2.5, ((0, 8), (2, 16)), jnp.float32),
        "first_moment": gaussian(key_of[4], (TENANTS, ADAPTER_RANK, W_AD), 1.0, 4.0, ((0, 8), (2, 16)), jnp.float32),
        "second_moment": jnp.clip(jnp.exp(math.log(2.0) - 2.3025851 * jax.random.uniform(key_of[5], (TENANTS, ADAPTER_RANK, W_AD), jnp.float32) ** block_scale(key_of[5], (TENANTS, ADAPTER_RANK, W_AD), ((0, 8), (2, 16)), -0.2, 0.2)), 0.2, 2.0),
        "tenant_home": draw_tenant_home(jax.random.fold_in(key_of[9], 71), 0),
        "read_tenants": draw_read_tenants(jax.random.fold_in(key_of[9], 71), 0),
        "row_tenant": draw_row_tenant(jax.random.fold_in(key_of[9], 71), 0),
    }


beta_first = 0.9
beta_second = 0.95
learn_rate = 0.1
adam_eps = 1e-08
corr_first = 1.0 - 0.9 ** 10
corr_second = 1.0 - 0.95 ** 10

def reference(tokens, cotangent, value_weight, adapters, first_moment, second_moment, tenant_home, read_tenants, row_tenant):
    device_count = N_TENANT * N_FSDP
    adapter_scale = 2.0 / math.sqrt(MODEL_WIDTH * ADAPTER_RANK)
    home_slots = jnp.take(tenant_home, read_tenants, axis=0).astype(jnp.int32)
    tok_blocks = tokens.reshape(device_count, TOK_DEV, MODEL_WIDTH)
    cot_blocks = cotangent.reshape(device_count, TOK_DEV, KV)
    row_blocks = row_tenant.reshape(device_count, TOK_DEV)

    def one_block(storage, block_items):
        tok_block, incoming_gradient_block, row_block, homes_here, read_block = block_items
        fetched_copy = jnp.take(adapters, homes_here, axis=0).astype(jnp.bfloat16)
        down_matrix_rows = fetched_copy[:, :, :MODEL_WIDTH].reshape(READS * ADAPTER_RANK, MODEL_WIDTH)
        up_matrix_rows = fetched_copy[:, :, MODEL_WIDTH:].reshape(READS * ADAPTER_RANK, KV)
        selected_tenants = (row_block[:, None] == read_block[None, :]).astype(jnp.float32)
        selected_tenants = jnp.repeat(selected_tenants, ADAPTER_RANK, axis=1)
        narrow_product = (jnp.dot(tok_block, down_matrix_rows.T, preferred_element_type=jnp.float32) * selected_tenants).astype(jnp.bfloat16)
        frozen_output = jnp.dot(tok_block, value_weight, preferred_element_type=jnp.float32)
        values = (frozen_output + adapter_scale * jnp.dot(narrow_product, up_matrix_rows, preferred_element_type=jnp.float32)).astype(jnp.bfloat16)
        narrow_gradient = (adapter_scale * jnp.dot(incoming_gradient_block, up_matrix_rows.T, preferred_element_type=jnp.float32) * selected_tenants).astype(jnp.bfloat16)
        back_base = jnp.dot(incoming_gradient_block, value_weight.T, preferred_element_type=jnp.float32)
        token_grad = (back_base + jnp.dot(narrow_gradient, down_matrix_rows, preferred_element_type=jnp.float32)).astype(jnp.bfloat16)
        grad_down = jnp.dot(narrow_gradient.T, tok_block, preferred_element_type=jnp.float32)
        up_gradient = adapter_scale * jnp.dot(narrow_product.T, incoming_gradient_block, preferred_element_type=jnp.float32)
        fetched_gradient = jnp.concatenate([grad_down, up_gradient], axis=1).reshape(READS, ADAPTER_RANK, W_AD)
        storage = storage.at[homes_here].add(fetched_gradient)
        return (storage, (values, token_grad))
    empty = jnp.zeros((TENANTS, ADAPTER_RANK, W_AD), jnp.float32)
    position_gradient, outputs = lax.scan(one_block, empty, (tok_blocks, cot_blocks, row_blocks, home_slots, read_tenants))
    values = outputs[0].reshape(ROWS, KV)
    token_grad = outputs[1].reshape(ROWS, MODEL_WIDTH)
    new_first = beta_first * first_moment + (1.0 - beta_first) * position_gradient
    new_second = beta_second * second_moment + (1.0 - beta_second) * position_gradient * position_gradient
    new_adapters = adapters - learn_rate * (new_first / corr_first) / (jnp.sqrt(new_second / corr_second) + adam_eps)
    refreshed = jnp.take(new_adapters, home_slots.reshape(-1), axis=0).astype(jnp.bfloat16)
    return (values, token_grad, new_adapters, new_first, new_second, refreshed)
```

```python
import functools
import math

import jax
import jax.numpy as jnp
from jax import lax
from jax.experimental import pallas as pl
from jax.experimental.pallas import tpu as pltpu
from jax.sharding import Mesh, PartitionSpec as P

beta_first = 0.9
beta_second = 0.95
learn_rate = 0.1
adam_eps = 1e-08
corr_first = 1.0 - 0.9**10
corr_second = 1.0 - 0.95**10

BF16 = jnp.bfloat16
F32 = jnp.float32
NT = (((1,), (1,)), ((), ()))
NN = (((1,), (0,)), ((), ()))
TN = (((0,), (0,)), ((), ()))
VMEM_LIMIT = 56 * 1024 * 1024
RANK = 16
SECTION = 576
PACK = 72
PAIR = 2 * SECTION


def lane_below(half):
    return lax.broadcasted_iota(jnp.int32, (8, 128), 1) < half


def pack_slice(row, odd):
    row = pltpu.roll(row, jnp.where(odd == 1, 576, 0), 1)
    low, high = row[0:8, 512:640], pltpu.roll(row[8:16, 512:640], 64, 1)
    first = lane_below(jnp.int32(64)) != (lax.broadcast(odd, (8, 128)) == 1)
    tail = jnp.where(first, low, high)
    return jnp.concatenate([row[:, 128 * j : 128 * j + 128] for j in range(4)] + [tail], axis=0)


def unpack_slice(block, odd):
    tail = block[64:72]
    last = jnp.concatenate([tail, pltpu.roll(tail, 64, 1)], axis=0)
    row = jnp.concatenate([block[16 * j : 16 * j + 16] for j in range(4)] + [last], axis=1)
    return pltpu.roll(row, jnp.where(odd == 1, 64, 0), 1)[:, :SECTION]


def middle_tile(even, odd):
    te, to = even.astype(F32)[64:72], odd.astype(F32)[64:72]
    below = lane_below(64)
    low = jnp.where(below, te, to)
    high = pltpu.roll(jnp.where(below, to, te), 64, 1)
    return jnp.concatenate([low, high], axis=0).astype(BF16)


def slot_of(home_ref, read_ref, d, tenant):
    return home_ref[read_ref[d, tenant]] - RANK * tenant


def pick_kernel(pos_ref, home_ref, read_ref, adapters_ref, out_ref, packed, wide):
    tenant, odd = pos_ref[0], pos_ref[1] & 1
    slots = adapters_ref.shape[0]

    def fill(h, _):
        wide[:, :SECTION] = adapters_ref[h]
        packed[h] = pack_slice(wide[...], odd)
        return 0

    lax.fori_loop(0, slots, fill, 0)

    def copy(d, _):
        out_ref[d] = packed[slot_of(home_ref, read_ref, d, tenant)].astype(BF16)
        return 0

    lax.fori_loop(0, out_ref.shape[0], copy, 0, unroll=4)


def pick(pos, home, read, adapters):
    slots, devices = adapters.shape[0], read.shape[0]
    return pl.pallas_call(
        pick_kernel,
        out_shape=jax.ShapeDtypeStruct((devices, PACK, 128), BF16),
        in_specs=[pl.BlockSpec(memory_space=pltpu.SMEM)] * 3 + [pl.BlockSpec(memory_space=pltpu.VMEM)],
        out_specs=pl.BlockSpec(memory_space=pltpu.VMEM),
        scratch_shapes=[pltpu.VMEM((slots, PACK, 128), F32), pltpu.VMEM((RANK, 640), F32)],
        compiler_params=pltpu.CompilerParams(vmem_limit_bytes=VMEM_LIMIT),
        cost_estimate=pl.CostEstimate(flops=0, bytes_accessed=6 * 2**20, transcendentals=0),
        name="pick",
    )(pos, home, read, adapters)


def lora_kernel(scale, pos_ref, read_ref, rows_ref, recv_ref, last_ref, tok_ref, cot_ref,
                send_ref, down_ref, low_ref, lg_ref, mask, lgt, low_acc, grad):
    j = pl.program_id(0)
    steps = pl.num_programs(0) - 1
    width = tok_ref.shape[1]
    reads = read_ref.shape[1]
    hidden = steps * width

    def assemble(block_ref, p):
        base = pl.multiple_of(p * PAIR, 128)
        for k in range(reads):
            even, odd = block_ref[k, 0], block_ref[k, 1]
            tiles = [even[16 * t : 16 * t + 16] for t in range(4)]
            tiles += [middle_tile(even, odd)]
            tiles += [odd[16 * t : 16 * t + 16] for t in range(4)]
            for t in range(9):
                down_ref[RANK * k : RANK * k + RANK, pl.ds(base + 128 * t, 128)] = tiles[t]

    @pl.when(j == 0)
    def _():
        assemble(last_ref, steps - 1)
        device = pos_ref[0] * 16 + pos_ref[1]
        owner = lax.broadcasted_iota(jnp.int32, mask.shape, 0) // RANK
        wanted = jnp.zeros(mask.shape, jnp.int32)
        for k in range(reads):
            wanted = jnp.where(owner == k, read_ref[device, k], wanted)
        mask[...] = (wanted == rows_ref[...]).astype(F32)
        up = down_ref[:, hidden:]
        grad_t = scale * lax.dot_general(up, cot_ref[...], NT, preferred_element_type=F32) * mask[...]
        lgt[...] = grad_t.astype(BF16)
        lg_ref[...] = grad_t.T.astype(BF16)
        low_acc[...] = jnp.zeros_like(low_acc)

    @pl.when(j < steps)
    def _():
        assemble(recv_ref, j)
        at = pl.multiple_of(j * width, 128)
        low_acc[...] += lax.dot_general(
            tok_ref[...], down_ref[:, pl.ds(at, width)], NT, preferred_element_type=F32
        )
        grad[:, pl.ds(at, width)] = lax.dot_general(
            lgt[...], tok_ref[...], NN, preferred_element_type=F32
        )

    @pl.when(j == steps)
    def _():
        low = (low_acc[...] * mask[...].T).astype(BF16)
        low_ref[...] = low
        grad[:, hidden:] = scale * lax.dot_general(low, cot_ref[...], TN, preferred_element_type=F32)

    @pl.when(j > 0)
    def _():
        base = pl.multiple_of((j - 1) * PAIR, 128)
        below = lane_below(64)
        for k in range(reads):
            tiles = [grad[RANK * k : RANK * k + RANK, pl.ds(base + 128 * t, 128)] for t in range(9)]
            low, high = tiles[4][0:8], pltpu.roll(tiles[4][8:16], 64, 1)
            send_ref[k, 0] = jnp.concatenate(tiles[:4] + [jnp.where(below, low, high)], axis=0).astype(BF16)
            send_ref[k, 1] = jnp.concatenate(tiles[5:] + [jnp.where(below, high, low)], axis=0).astype(BF16)


def lora(scale, pos, read, rows, recv, tokens, cotangent):
    n, hidden = tokens.shape
    kv = cotangent.shape[1]
    reads = read.shape[1]
    ranks = reads * RANK
    shards = (hidden + kv) // SECTION
    steps = shards // 2
    width = hidden // steps
    recv = recv.reshape(reads, shards, PACK, 128)
    block = (reads, 2, PACK, 128)
    last = steps - 1
    smem = pl.BlockSpec(memory_space=pltpu.SMEM)
    return pl.pallas_call(
        functools.partial(lora_kernel, scale),
        grid=(steps + 1,),
        out_shape=(
            jax.ShapeDtypeStruct(recv.shape, BF16),
            jax.ShapeDtypeStruct((ranks, hidden + kv), BF16),
            jax.ShapeDtypeStruct((n, ranks), BF16),
            jax.ShapeDtypeStruct((n, ranks), BF16),
        ),
        in_specs=[
            smem,
            smem,
            pl.BlockSpec((1, n), lambda j: (0, 0)),
            pl.BlockSpec(block, lambda j: (0, jnp.minimum(j, last), 0, 0)),
            pl.BlockSpec(block, lambda j: (0, last, 0, 0)),
            pl.BlockSpec((n, width), lambda j: (0, jnp.minimum(j, last))),
            pl.BlockSpec((n, kv), lambda j: (0, 0)),
        ],
        out_specs=(
            pl.BlockSpec(block, lambda j: (0, jnp.maximum(j - 1, 0), 0, 0)),
            pl.BlockSpec((ranks, hidden + kv), lambda j: (0, 0)),
            pl.BlockSpec((n, ranks), lambda j: (0, 0)),
            pl.BlockSpec((n, ranks), lambda j: (0, 0)),
        ),
        scratch_shapes=[
            pltpu.VMEM((ranks, n), F32),
            pltpu.VMEM((ranks, n), BF16),
            pltpu.VMEM((n, ranks), F32),
            pltpu.VMEM((ranks, hidden + kv), F32),
        ],
        compiler_params=pltpu.CompilerParams(vmem_limit_bytes=VMEM_LIMIT),
        cost_estimate=pl.CostEstimate(flops=2**32, bytes_accessed=16 * 2**20, transcendentals=0),
        name="lora",
    )(pos, read, rows, recv, recv, tokens, cotangent)


def adam_kernel(pos_ref, home_ref, read_ref, recv_ref, a_ref, m_ref, v_ref,
                send_ref, new_a_ref, new_m_ref, new_v_ref, acc, packed, wide):
    step = pl.program_id(0)
    tenant, odd = pos_ref[0], pos_ref[1] & 1
    devices = recv_ref.shape[0]
    here = a_ref.shape[0]

    @pl.when(step == 0)
    def _():
        acc[...] = jnp.zeros_like(acc)

        def add(d, _):
            acc[slot_of(home_ref, read_ref, d, tenant)] += recv_ref[d].astype(F32)
            return 0

        lax.fori_loop(0, devices, add, 0, unroll=4)

    def update(i, _):
        h = step * here + i
        g = unpack_slice(acc[h], odd)
        new_m = beta_first * m_ref[i] + (1.0 - beta_first) * g
        new_v = beta_second * v_ref[i] + (1.0 - beta_second) * g * g
        new_a = a_ref[i] - learn_rate * (new_m / corr_first) / (
            jnp.sqrt(new_v / corr_second) + adam_eps
        )
        new_m_ref[i] = new_m
        new_v_ref[i] = new_v
        new_a_ref[i] = new_a
        wide[:, :SECTION] = new_a
        packed[h] = pack_slice(wide[...], odd)
        return 0

    lax.fori_loop(0, here, update, 0)

    @pl.when(step == pl.num_programs(0) - 1)
    def _():
        def copy(d, _):
            send_ref[d] = packed[slot_of(home_ref, read_ref, d, tenant)].astype(BF16)
            return 0

        lax.fori_loop(0, devices, copy, 0, unroll=4)


def adam(pos, home, read, recv, adapters, first, second):
    slots = adapters.shape[0]
    steps = 4
    smem = pl.BlockSpec(memory_space=pltpu.SMEM)
    whole = pl.BlockSpec(recv.shape, lambda i: (0, 0, 0))
    part = pl.BlockSpec((slots // steps,) + adapters.shape[1:], lambda i: (i, 0, 0))
    stored = jax.ShapeDtypeStruct(adapters.shape, F32)
    return pl.pallas_call(
        adam_kernel,
        grid=(steps,),
        out_shape=(jax.ShapeDtypeStruct(recv.shape, BF16), stored, stored, stored),
        in_specs=[smem, smem, smem, whole, part, part, part],
        out_specs=(whole, part, part, part),
        scratch_shapes=[
            pltpu.VMEM((slots, PACK, 128), F32),
            pltpu.VMEM((slots, PACK, 128), F32),
            pltpu.VMEM((RANK, 640), F32),
        ],
        compiler_params=pltpu.CompilerParams(vmem_limit_bytes=VMEM_LIMIT),
        cost_estimate=pl.CostEstimate(flops=2**24, bytes_accessed=20 * 2**20, transcendentals=0),
        name="adam",
    )(pos, home, read, recv, adapters, first, second)


def refresh_kernel(recv_ref, out_ref):
    for p in range(recv_ref.shape[1] // 2):
        even, odd = recv_ref[0, 2 * p], recv_ref[0, 2 * p + 1]
        tiles = [even[16 * t : 16 * t + 16] for t in range(4)]
        tiles += [middle_tile(even, odd)]
        tiles += [odd[16 * t : 16 * t + 16] for t in range(4)]
        for t in range(9):
            out_ref[0, :, PAIR * p + 128 * t : PAIR * p + 128 * t + 128] = tiles[t]


def refresh(recv, reads):
    shards = recv.shape[0] // reads
    recv = recv.reshape(reads, shards, PACK, 128)
    return pl.pallas_call(
        refresh_kernel,
        grid=(reads,),
        out_shape=jax.ShapeDtypeStruct((reads, RANK, shards * SECTION), BF16),
        in_specs=[pl.BlockSpec((1, shards, PACK, 128), lambda k: (k, 0, 0, 0))],
        out_specs=pl.BlockSpec((1, RANK, shards * SECTION), lambda k: (k, 0, 0)),
        compiler_params=pltpu.CompilerParams(vmem_limit_bytes=VMEM_LIMIT),
        cost_estimate=pl.CostEstimate(flops=0, bytes_accessed=5 * 2**20, transcendentals=0),
        name="refresh",
    )(recv)


def base_kernel(scale, final, half_ref, w_ref, tok_ref, cot_ref, down_ref, up_ref, low_ref, lg_ref, *rest):
    if final:
        part_ref, _, tg_ref, values_ref, acc = rest
    else:
        tg_ref, values_ref, acc = rest
    i = pl.program_id(0)
    term = jnp.dot(tok_ref[...], w_ref[...], preferred_element_type=F32)

    @pl.when(i == 0)
    def _():
        if final:
            acc[...] = part_ref[...] + term
        else:
            acc[...] = term + scale * jnp.dot(low_ref[...], up_ref[...], preferred_element_type=F32)

    @pl.when(i > 0)
    def _():
        acc[...] += term

    tg_ref[...] = (
        lax.dot_general(cot_ref[...], w_ref[...], NT, preferred_element_type=F32)
        + jnp.dot(lg_ref[...], down_ref[...], preferred_element_type=F32)
    ).astype(BF16)

    @pl.when(i == pl.num_programs(0) - 1)
    def _():
        values_ref[...] = acc[...].astype(values_ref.dtype)


def base(scale, half, w_half, tokens, cotangent, down, low, lg, part=None, grad=None):
    final = part is not None
    n, hidden = tokens.shape
    kv = cotangent.shape[1]
    ranks = low.shape[1]
    rows = 256
    steps = w_half.shape[0] // rows
    in_specs = [
        pl.BlockSpec((rows, kv), lambda i, h: (i, 0)),
        pl.BlockSpec((n, rows), lambda i, h: (0, 2 * i + h[0])),
        pl.BlockSpec((n, kv), lambda i, h: (0, 0)),
        pl.BlockSpec((ranks, rows), lambda i, h: (0, 2 * i + h[0])),
        pl.BlockSpec((ranks, kv), lambda i, h: (0, hidden // kv)),
        pl.BlockSpec((n, ranks), lambda i, h: (0, 0)),
        pl.BlockSpec((n, ranks), lambda i, h: (0, 0)),
    ]
    args = [half, w_half, tokens, cotangent, down, down, low, lg]
    aliases = {}
    if final:
        in_specs += [pl.BlockSpec((n, kv), lambda i, h: (0, 0)), pl.BlockSpec(memory_space=pl.ANY)]
        args += [part, grad]
        aliases = {len(args) - 1: 0}
    return pl.pallas_call(
        functools.partial(base_kernel, scale, final),
        grid_spec=pltpu.PrefetchScalarGridSpec(
            num_scalar_prefetch=1,
            grid=(steps,),
            in_specs=in_specs,
            out_specs=(
                pl.BlockSpec((n, rows), lambda i, h: (0, 2 * i + h[0])),
                pl.BlockSpec((n, kv), lambda i, h: (0, 0)),
            ),
            scratch_shapes=[pltpu.VMEM((n, kv), F32)],
        ),
        out_shape=(
            jax.ShapeDtypeStruct((n, hidden), BF16),
            jax.ShapeDtypeStruct((n, kv), BF16 if final else F32),
        ),
        input_output_aliases=aliases,
        compiler_params=pltpu.CompilerParams(vmem_limit_bytes=VMEM_LIMIT),
        cost_estimate=pl.CostEstimate(flops=9 * 2**30, bytes_accessed=20 * 2**20, transcendentals=0),
        name="base_final" if final else "base_first",
    )(*args)


def exchange(blocks):
    return lax.all_to_all(blocks, ("x", "core", "fsdp"), split_axis=0, concat_axis=0, tiled=True)


def per_device(
    tokens,
    cotangent,
    value_weight,
    adapters,
    first_moment,
    second_moment,
    tenant_home,
    read_tenants,
    row_tenant,
):
    hidden = tokens.shape[1]
    reads = read_tenants.shape[1]
    core = lax.axis_index("core").astype(jnp.int32)
    tenant = 2 * lax.axis_index("x").astype(jnp.int32) + core
    pos = jnp.stack([tenant, lax.axis_index("fsdp").astype(jnp.int32)])
    scale = 2.0 / math.sqrt(hidden * RANK)

    half_rows = value_weight.shape[0] // 2
    mine = lax.dynamic_slice_in_dim(value_weight, core * half_rows, half_rows, 0)
    w_mine = lax.all_gather(mine, "fsdp", axis=0, tiled=True)
    w_other = lax.ppermute(w_mine, "core", [(0, 1), (1, 0)])

    fetched = exchange(pick(pos, tenant_home, read_tenants, adapters))
    send, down, low, lg = lora(
        scale, pos, read_tenants, row_tenant.reshape(1, -1), fetched, tokens, cotangent
    )
    received = exchange(send.reshape(fetched.shape))
    fresh, new_adapters, new_first, new_second = adam(
        pos, tenant_home, read_tenants, received, adapters, first_moment, second_moment
    )
    refreshed = refresh(exchange(fresh), reads)

    grad, part = base(scale, core[None], w_mine, tokens, cotangent, down, low, lg)
    token_grad, values = base(
        scale, 1 - core[None], w_other, tokens, cotangent, down, low, lg, part, grad
    )
    return (values, token_grad, new_adapters, new_first, new_second, refreshed)


def solution(mesh):
    shape = mesh.devices.shape
    inner = Mesh(mesh.devices.reshape(shape[0] // 2, 2, shape[1]), ("x", "core", "fsdp"))
    rows = ("x", "core", "fsdp")
    tenant = ("x", "core")
    return jax.shard_map(
        per_device,
        mesh=inner,
        in_specs=(
            P(rows, None),
            P(rows, None),
            P("fsdp", None),
            P(tenant, None, "fsdp"),
            P(tenant, None, "fsdp"),
            P(tenant, None, "fsdp"),
            P(),
            P(),
            P(rows),
        ),
        out_specs=(
            P(rows, None),
            P(rows, None),
            P(tenant, None, "fsdp"),
            P(tenant, None, "fsdp"),
            P(tenant, None, "fsdp"),
            P(rows, None, None),
        ),
        check_vma=False,
    )
```

```python
import functools
import math

import jax
import jax.numpy as jnp
from jax import lax
from jax.experimental import pallas as pl
from jax.experimental.pallas import tpu as pltpu
from jax.sharding import Mesh, PartitionSpec as P

beta_first = 0.9
beta_second = 0.95
learn_rate = 0.1
adam_eps = 1e-08
corr_first = 1.0 - 0.9**10
corr_second = 1.0 - 0.95**10

BF16 = jnp.bfloat16
F32 = jnp.float32
NT = (((1,), (1,)), ((), ()))
NN = (((1,), (0,)), ((), ()))
TN = (((0,), (0,)), ((), ()))
VMEM_LIMIT = 56 * 1024 * 1024
RANK = 16
SECTION = 576
PACK = 72
PAIR = 2 * SECTION


def lane_below(half):
    return lax.broadcasted_iota(jnp.int32, (8, 128), 1) < half


def pack_slice(row, odd):
    row = pltpu.roll(row, jnp.where(odd == 1, 576, 0), 1)
    low, high = row[0:8, 512:640], pltpu.roll(row[8:16, 512:640], 64, 1)
    first = lane_below(jnp.int32(64)) != (lax.broadcast(odd, (8, 128)) == 1)
    tail = jnp.where(first, low, high)
    return jnp.concatenate([row[:, 128 * j : 128 * j + 128] for j in range(4)] + [tail], axis=0)


def unpack_slice(block, odd):
    tail = block[64:72]
    last = jnp.concatenate([tail, pltpu.roll(tail, 64, 1)], axis=0)
    row = jnp.concatenate([block[16 * j : 16 * j + 16] for j in range(4)] + [last], axis=1)
    return pltpu.roll(row, jnp.where(odd == 1, 64, 0), 1)[:, :SECTION]


def middle_tile(even, odd):
    te, to = even.astype(F32)[64:72], odd.astype(F32)[64:72]
    below = lane_below(64)
    low = jnp.where(below, te, to)
    high = pltpu.roll(jnp.where(below, to, te), 64, 1)
    return jnp.concatenate([low, high], axis=0).astype(BF16)


def slot_of(home_ref, read_ref, d, tenant):
    return home_ref[read_ref[d, tenant]] - RANK * tenant


def pick_kernel(pos_ref, home_ref, read_ref, adapters_ref, out_ref, packed, wide):
    tenant, odd = pos_ref[0], pos_ref[1] & 1
    slots = adapters_ref.shape[0]

    def fill(h, _):
        wide[:, :SECTION] = adapters_ref[h]
        packed[h] = pack_slice(wide[...], odd)
        return 0

    lax.fori_loop(0, slots, fill, 0)

    def copy(d, _):
        out_ref[d] = packed[slot_of(home_ref, read_ref, d, tenant)].astype(BF16)
        return 0

    lax.fori_loop(0, out_ref.shape[0], copy, 0, unroll=4)


def pick(pos, home, read, adapters):
    slots, devices = adapters.shape[0], read.shape[0]
    return pl.pallas_call(
        pick_kernel,
        out_shape=jax.ShapeDtypeStruct((devices, PACK, 128), BF16),
        in_specs=[pl.BlockSpec(memory_space=pltpu.SMEM)] * 3 + [pl.BlockSpec(memory_space=pltpu.VMEM)],
        out_specs=pl.BlockSpec(memory_space=pltpu.VMEM),
        scratch_shapes=[pltpu.VMEM((slots, PACK, 128), F32), pltpu.VMEM((RANK, 640), F32)],
        compiler_params=pltpu.CompilerParams(vmem_limit_bytes=VMEM_LIMIT),
        cost_estimate=pl.CostEstimate(flops=0, bytes_accessed=6 * 2**20, transcendentals=0),
        name="pick",
    )(pos, home, read, adapters)


def lora_kernel(scale, pos_ref, read_ref, rows_ref, recv_ref, last_ref, tok_ref, cot_ref,
                send_ref, down_ref, low_ref, lg_ref, mask, lgt, low_acc, grad):
    j = pl.program_id(0)
    steps = pl.num_programs(0) - 1
    width = tok_ref.shape[1]
    reads = read_ref.shape[1]
    hidden = steps * width

    def assemble(block_ref, p):
        base = pl.multiple_of(p * PAIR, 128)
        for k in range(reads):
            even, odd = block_ref[k, 0], block_ref[k, 1]
            tiles = [even[16 * t : 16 * t + 16] for t in range(4)]
            tiles += [middle_tile(even, odd)]
            tiles += [odd[16 * t : 16 * t + 16] for t in range(4)]
            for t in range(9):
                down_ref[RANK * k : RANK * k + RANK, pl.ds(base + 128 * t, 128)] = tiles[t]

    @pl.when(j == 0)
    def _():
        assemble(last_ref, steps - 1)
        device = pos_ref[0] * 16 + pos_ref[1]
        owner = lax.broadcasted_iota(jnp.int32, mask.shape, 0) // RANK
        wanted = jnp.zeros(mask.shape, jnp.int32)
        for k in range(reads):
            wanted = jnp.where(owner == k, read_ref[device, k], wanted)
        mask[...] = (wanted == rows_ref[...]).astype(F32)
        up = down_ref[:, hidden:]
        grad_t = scale * lax.dot_general(up, cot_ref[...], NT, preferred_element_type=F32) * mask[...]
        lgt[...] = grad_t.astype(BF16)
        lg_ref[...] = grad_t.T.astype(BF16)
        low_acc[...] = jnp.zeros_like(low_acc)

    @pl.when(j < steps)
    def _():
        assemble(recv_ref, j)
        at = pl.multiple_of(j * width, 128)
        low_acc[...] += lax.dot_general(
            tok_ref[...], down_ref[:, pl.ds(at, width)], NT, preferred_element_type=F32
        )
        grad[:, pl.ds(at, width)] = lax.dot_general(
            lgt[...], tok_ref[...], NN, preferred_element_type=F32
        )

    @pl.when(j == steps)
    def _():
        low = (low_acc[...] * mask[...].T).astype(BF16)
        low_ref[...] = low
        grad[:, hidden:] = scale * lax.dot_general(low, cot_ref[...], TN, preferred_element_type=F32)

    @pl.when(j > 0)
    def _():
        base = pl.multiple_of((j - 1) * PAIR, 128)
        below = lane_below(64)
        for k in range(reads):
            tiles = [grad[RANK * k : RANK * k + RANK, pl.ds(base + 128 * t, 128)] for t in range(9)]
            low, high = tiles[4][0:8], pltpu.roll(tiles[4][8:16], 64, 1)
            send_ref[k, 0] = jnp.concatenate(tiles[:4] + [jnp.where(below, low, high)], axis=0).astype(BF16)
            send_ref[k, 1] = jnp.concatenate(tiles[5:] + [jnp.where(below, high, low)], axis=0).astype(BF16)


def lora(scale, pos, read, rows, recv, tokens, cotangent):
    n, hidden = tokens.shape
    kv = cotangent.shape[1]
    reads = read.shape[1]
    ranks = reads * RANK
    shards = (hidden + kv) // SECTION
    steps = shards // 2
    width = hidden // steps
    recv = recv.reshape(reads, shards, PACK, 128)
    block = (reads, 2, PACK, 128)
    last = steps - 1
    smem = pl.BlockSpec(memory_space=pltpu.SMEM)
    return pl.pallas_call(
        functools.partial(lora_kernel, scale),
        grid=(steps + 1,),
        out_shape=(
            jax.ShapeDtypeStruct(recv.shape, BF16),
            jax.ShapeDtypeStruct((ranks, hidden + kv), BF16),
            jax.ShapeDtypeStruct((n, ranks), BF16),
            jax.ShapeDtypeStruct((n, ranks), BF16),
        ),
        in_specs=[
            smem,
            smem,
            pl.BlockSpec((1, n), lambda j: (0, 0)),
            pl.BlockSpec(block, lambda j: (0, jnp.minimum(j, last), 0, 0)),
            pl.BlockSpec(block, lambda j: (0, last, 0, 0)),
            pl.BlockSpec((n, width), lambda j: (0, jnp.minimum(j, last))),
            pl.BlockSpec((n, kv), lambda j: (0, 0)),
        ],
        out_specs=(
            pl.BlockSpec(block, lambda j: (0, jnp.maximum(j - 1, 0), 0, 0)),
            pl.BlockSpec((ranks, hidden + kv), lambda j: (0, 0)),
            pl.BlockSpec((n, ranks), lambda j: (0, 0)),
            pl.BlockSpec((n, ranks), lambda j: (0, 0)),
        ),
        scratch_shapes=[
            pltpu.VMEM((ranks, n), F32),
            pltpu.VMEM((ranks, n), BF16),
            pltpu.VMEM((n, ranks), F32),
            pltpu.VMEM((ranks, hidden + kv), F32),
        ],
        compiler_params=pltpu.CompilerParams(vmem_limit_bytes=VMEM_LIMIT),
        cost_estimate=pl.CostEstimate(flops=2**32, bytes_accessed=16 * 2**20, transcendentals=0),
        name="lora",
    )(pos, read, rows, recv, recv, tokens, cotangent)


def adam_kernel(pos_ref, home_ref, read_ref, recv_ref, a_ref, m_ref, v_ref,
                send_ref, new_a_ref, new_m_ref, new_v_ref, acc, packed, wide):
    step = pl.program_id(0)
    tenant, odd = pos_ref[0], pos_ref[1] & 1
    devices = recv_ref.shape[0]
    here = a_ref.shape[0]

    @pl.when(step == 0)
    def _():
        acc[...] = jnp.zeros_like(acc)

        def add(d, _):
            acc[slot_of(home_ref, read_ref, d, tenant)] += recv_ref[d].astype(F32)
            return 0

        lax.fori_loop(0, devices, add, 0, unroll=4)

    def update(i, _):
        h = step * here + i
        g = unpack_slice(acc[h], odd)
        new_m = beta_first * m_ref[i] + (1.0 - beta_first) * g
        new_v = beta_second * v_ref[i] + (1.0 - beta_second) * g * g
        new_a = a_ref[i] - learn_rate * (new_m / corr_first) / (
            jnp.sqrt(new_v / corr_second) + adam_eps
        )
        new_m_ref[i] = new_m
        new_v_ref[i] = new_v
        new_a_ref[i] = new_a
        wide[:, :SECTION] = new_a
        packed[h] = pack_slice(wide[...], odd)
        return 0

    lax.fori_loop(0, here, update, 0)

    @pl.when(step == pl.num_programs(0) - 1)
    def _():
        def copy(d, _):
            send_ref[d] = packed[slot_of(home_ref, read_ref, d, tenant)].astype(BF16)
            return 0

        lax.fori_loop(0, devices, copy, 0, unroll=4)


def adam(pos, home, read, recv, adapters, first, second):
    slots = adapters.shape[0]
    steps = 4
    smem = pl.BlockSpec(memory_space=pltpu.SMEM)
    whole = pl.BlockSpec(recv.shape, lambda i: (0, 0, 0))
    part = pl.BlockSpec((slots // steps,) + adapters.shape[1:], lambda i: (i, 0, 0))
    stored = jax.ShapeDtypeStruct(adapters.shape, F32)
    return pl.pallas_call(
        adam_kernel,
        grid=(steps,),
        out_shape=(jax.ShapeDtypeStruct(recv.shape, BF16), stored, stored, stored),
        in_specs=[smem, smem, smem, whole, part, part, part],
        out_specs=(whole, part, part, part),
        scratch_shapes=[
            pltpu.VMEM((slots, PACK, 128), F32),
            pltpu.VMEM((slots, PACK, 128), F32),
            pltpu.VMEM((RANK, 640), F32),
        ],
        compiler_params=pltpu.CompilerParams(vmem_limit_bytes=VMEM_LIMIT),
        cost_estimate=pl.CostEstimate(flops=2**24, bytes_accessed=20 * 2**20, transcendentals=0),
        name="adam",
    )(pos, home, read, recv, adapters, first, second)


def refresh_kernel(recv_ref, out_ref):
    for p in range(recv_ref.shape[1] // 2):
        even, odd = recv_ref[0, 2 * p], recv_ref[0, 2 * p + 1]
        tiles = [even[16 * t : 16 * t + 16] for t in range(4)]
        tiles += [middle_tile(even, odd)]
        tiles += [odd[16 * t : 16 * t + 16] for t in range(4)]
        for t in range(9):
            out_ref[0, :, PAIR * p + 128 * t : PAIR * p + 128 * t + 128] = tiles[t]


def refresh(recv, reads):
    shards = recv.shape[0] // reads
    recv = recv.reshape(reads, shards, PACK, 128)
    return pl.pallas_call(
        refresh_kernel,
        grid=(reads,),
        out_shape=jax.ShapeDtypeStruct((reads, RANK, shards * SECTION), BF16),
        in_specs=[pl.BlockSpec((1, shards, PACK, 128), lambda k: (k, 0, 0, 0))],
        out_specs=pl.BlockSpec((1, RANK, shards * SECTION), lambda k: (k, 0, 0)),
        compiler_params=pltpu.CompilerParams(vmem_limit_bytes=VMEM_LIMIT),
        cost_estimate=pl.CostEstimate(flops=0, bytes_accessed=5 * 2**20, transcendentals=0),
        name="refresh",
    )(recv)


def base_kernel(scale, final, half_ref, w_ref, *rest):
    toks, downs, rest = rest[:4], rest[4:8], rest[8:]
    cot_ref, up_ref, low_ref, lg_ref, *rest = rest
    if final:
        part_ref, _, tg_ref, values_ref, row, down, acc, out, sems = rest
    else:
        tg_ref, values_ref, row, down, acc, out, sems = rest
    i = pl.program_id(0)
    steps = pl.num_programs(0)
    cols = row.shape[1] // 4
    slot = lax.rem(i, 2)

    def copies(step, at):
        for t in range(4):
            start = pl.multiple_of((2 * (4 * step + t) + half_ref[0]) * cols, cols)
            yield pltpu.make_async_copy(out.at[at, t], tg_ref.at[:, pl.ds(start, cols)], sems.at[at, t])

    @pl.when(i == 0)
    def _():
        if final:
            acc[...] = part_ref[...]
        else:
            acc[...] = scale * jnp.dot(low_ref[...], up_ref[...], preferred_element_type=F32)

    @pl.when(i >= 2)
    def _():
        for copy in copies(i - 2, slot):
            copy.wait()

    for t in range(4):
        row[:, cols * t : cols * t + cols] = toks[t][...]
        down[:, cols * t : cols * t + cols] = downs[t][...]
    acc[...] += jnp.dot(row[...], w_ref[...], preferred_element_type=F32)
    grad = lax.dot_general(cot_ref[...], w_ref[...], NT, preferred_element_type=F32) + jnp.dot(
        lg_ref[...], down[...], preferred_element_type=F32
    )
    for t in range(4):
        out[slot, t] = grad[:, cols * t : cols * t + cols].astype(BF16)
    for copy in copies(i, slot):
        copy.start()

    @pl.when(i == steps - 1)
    def _():
        values_ref[...] = acc[...].astype(values_ref.dtype)
        for copy in copies(i - 1, 1 - slot):
            copy.wait()
        for copy in copies(i, slot):
            copy.wait()


def base(scale, half, w_half, tokens, cotangent, down, low, lg, part=None, grad=None):
    final = part is not None
    n, hidden = tokens.shape
    kv = cotangent.shape[1]
    ranks = low.shape[1]
    rows = 256
    steps = w_half.shape[0] // (4 * rows)
    in_specs = [pl.BlockSpec((4 * rows, kv), lambda i, h: (i, 0))]
    for height in (n, ranks):
        for t in range(4):
            in_specs.append(
                pl.BlockSpec((height, rows), lambda i, h, t=t: (0, 2 * (4 * i + t) + h[0]))
            )
    in_specs += [
        pl.BlockSpec((n, kv), lambda i, h: (0, 0)),
        pl.BlockSpec((ranks, kv), lambda i, h: (0, hidden // kv)),
        pl.BlockSpec((n, ranks), lambda i, h: (0, 0)),
        pl.BlockSpec((n, ranks), lambda i, h: (0, 0)),
    ]
    args = [half, w_half] + [tokens] * 4 + [down] * 4 + [cotangent, down, low, lg]
    aliases = {}
    if final:
        in_specs += [pl.BlockSpec((n, kv), lambda i, h: (0, 0)), pl.BlockSpec(memory_space=pl.ANY)]
        args += [part, grad]
        aliases = {len(args) - 1: 0}
    return pl.pallas_call(
        functools.partial(base_kernel, scale, final),
        grid_spec=pltpu.PrefetchScalarGridSpec(
            num_scalar_prefetch=1,
            grid=(steps,),
            in_specs=in_specs,
            out_specs=(
                pl.BlockSpec(memory_space=pl.ANY),
                pl.BlockSpec((n, kv), lambda i, h: (0, 0)),
            ),
            scratch_shapes=[
                pltpu.VMEM((n, 4 * rows), BF16),
                pltpu.VMEM((ranks, 4 * rows), BF16),
                pltpu.VMEM((n, kv), F32),
                pltpu.VMEM((2, 4, n, rows), BF16),
                pltpu.SemaphoreType.DMA((2, 4)),
            ],
        ),
        out_shape=(
            jax.ShapeDtypeStruct((n, hidden), BF16),
            jax.ShapeDtypeStruct((n, kv), BF16 if final else F32),
        ),
        input_output_aliases=aliases,
        compiler_params=pltpu.CompilerParams(vmem_limit_bytes=VMEM_LIMIT),
        cost_estimate=pl.CostEstimate(flops=9 * 2**30, bytes_accessed=20 * 2**20, transcendentals=0),
        name="base_final" if final else "base_first",
    )(*args)


def exchange(blocks):
    return lax.all_to_all(blocks, ("x", "core", "fsdp"), split_axis=0, concat_axis=0, tiled=True)


def per_device(
    tokens,
    cotangent,
    value_weight,
    adapters,
    first_moment,
    second_moment,
    tenant_home,
    read_tenants,
    row_tenant,
):
    hidden = tokens.shape[1]
    reads = read_tenants.shape[1]
    core = lax.axis_index("core").astype(jnp.int32)
    tenant = 2 * lax.axis_index("x").astype(jnp.int32) + core
    pos = jnp.stack([tenant, lax.axis_index("fsdp").astype(jnp.int32)])
    scale = 2.0 / math.sqrt(hidden * RANK)

    half_rows = value_weight.shape[0] // 2
    mine = lax.dynamic_slice_in_dim(value_weight, core * half_rows, half_rows, 0)
    w_mine = lax.all_gather(mine, "fsdp", axis=0, tiled=True)

    fetched = exchange(pick(pos, tenant_home, read_tenants, adapters))
    send, down, low, lg = lora(
        scale, pos, read_tenants, row_tenant.reshape(1, -1), fetched, tokens, cotangent
    )
    received = exchange(send.reshape(fetched.shape))
    w_mine, received = lax.optimization_barrier((w_mine, received))
    w_other = lax.ppermute(w_mine, "core", [(0, 1), (1, 0)])
    fresh, new_adapters, new_first, new_second = adam(
        pos, tenant_home, read_tenants, received, adapters, first_moment, second_moment
    )
    w_mine, fresh = lax.optimization_barrier((w_mine, fresh))
    renewed = exchange(fresh)
    grad, part = base(scale, core[None], w_mine, tokens, cotangent, down, low, lg)
    token_grad, values = base(
        scale, 1 - core[None], w_other, tokens, cotangent, down, low, lg, part, grad
    )
    values, renewed = lax.optimization_barrier((values, renewed))
    refreshed = refresh(renewed, reads)
    return (values, token_grad, new_adapters, new_first, new_second, refreshed)


def solution(mesh):
    shape = mesh.devices.shape
    inner = Mesh(mesh.devices.reshape(shape[0] // 2, 2, shape[1]), ("x", "core", "fsdp"))
    rows = ("x", "core", "fsdp")
    tenant = ("x", "core")
    return jax.shard_map(
        per_device,
        mesh=inner,
        in_specs=(
            P(rows, None),
            P(rows, None),
            P("fsdp", None),
            P(tenant, None, "fsdp"),
            P(tenant, None, "fsdp"),
            P(tenant, None, "fsdp"),
            P(),
            P(),
            P(rows),
        ),
        out_specs=(
            P(rows, None),
            P(rows, None),
            P(tenant, None, "fsdp"),
            P(tenant, None, "fsdp"),
            P(tenant, None, "fsdp"),
            P(rows, None, None),
        ),
        check_vma=False,
    )
```

```python
import functools
import math

import jax
import jax.numpy as jnp
from jax import lax
from jax.experimental import pallas as pl
from jax.experimental.pallas import tpu as pltpu
from jax.sharding import Mesh, PartitionSpec as P

beta_first = 0.9
beta_second = 0.95
learn_rate = 0.1
adam_eps = 1e-08
corr_first = 1.0 - 0.9**10
corr_second = 1.0 - 0.95**10

BF16 = jnp.bfloat16
F32 = jnp.float32
NT = (((1,), (1,)), ((), ()))
NN = (((1,), (0,)), ((), ()))
TN = (((0,), (0,)), ((), ()))
VMEM_LIMIT = 56 * 1024 * 1024
RANK = 16
SECTION = 576
PACK = 72
PAIR = 2 * SECTION


def lane_below(half):
    return lax.broadcasted_iota(jnp.int32, (8, 128), 1) < half


def halves(low, high):
    return jnp.where(lax.broadcasted_iota(jnp.int32, low.shape, 1) < 64, low, high)


def pack_slice(tiles, odd):
    rolled = [pltpu.roll(t, 64, 1) for t in tiles]
    body = [jnp.where(odd, halves(rolled[j], rolled[j + 1]), tiles[j]) for j in range(4)]
    tail = jnp.where(
        odd,
        halves(tiles[0][8:16], rolled[0][0:8]),
        halves(tiles[4][0:8], rolled[4][8:16]),
    )
    return jnp.concatenate(body + [tail], axis=0)


def unpack_slice(block, odd):
    tail = block[64:72]
    tail_rolled = pltpu.roll(tail, 64, 1)
    tiles = [block[16 * j : 16 * j + 16] for j in range(4)]
    rolled = [pltpu.roll(t, 64, 1) for t in tiles]
    last = jnp.concatenate([tail, tail_rolled], axis=0)
    before = jnp.concatenate([tail_rolled, tail], axis=0)
    row = [jnp.where(odd, halves(before, rolled[0]), tiles[0])]
    row += [jnp.where(odd, halves(rolled[j - 1], rolled[j]), tiles[j]) for j in range(1, 4)]
    return row + [jnp.where(odd, rolled[3], last)]


def load_tiles(ref, h):
    tail = jnp.concatenate([ref[h, :, 512:SECTION], jnp.zeros((RANK, 640 - SECTION), F32)], axis=1)
    return [ref[h, :, 128 * j : 128 * j + 128] for j in range(4)] + [tail]


def store_tiles(ref, h, tiles):
    for j in range(4):
        ref[h, :, 128 * j : 128 * j + 128] = tiles[j]
    ref[h, :, 512:SECTION] = tiles[4][:, : SECTION - 512]


def middle_tile(even, odd):
    te, to = even.astype(F32)[64:72], odd.astype(F32)[64:72]
    below = lane_below(64)
    low = jnp.where(below, te, to)
    high = pltpu.roll(jnp.where(below, to, te), 64, 1)
    return jnp.concatenate([low, high], axis=0).astype(BF16)


def slot_of(home_ref, read_ref, d, tenant):
    return home_ref[read_ref[d, tenant]] - RANK * tenant


def pick_kernel(pos_ref, home_ref, read_ref, adapters_ref, out_ref, packed):
    step = pl.program_id(0)
    tenant, odd = pos_ref[0], (pos_ref[1] & 1) == 1
    slots, here = adapters_ref.shape[0], out_ref.shape[0]

    @pl.when(step == 0)
    def _():
        def fill(h, _):
            packed[h] = pack_slice(load_tiles(adapters_ref, h), odd).astype(BF16)
            return 0

        lax.fori_loop(0, slots, fill, 0, unroll=2)

    def copy(d, _):
        out_ref[d] = packed[slot_of(home_ref, read_ref, step * here + d, tenant)]
        return 0

    lax.fori_loop(0, here, copy, 0, unroll=8)


def pick(pos, home, read, adapters):
    slots, devices = adapters.shape[0], read.shape[0]
    steps = 2
    return pl.pallas_call(
        pick_kernel,
        grid=(steps,),
        out_shape=jax.ShapeDtypeStruct((devices, PACK, 128), BF16),
        in_specs=[pl.BlockSpec(memory_space=pltpu.SMEM)] * 3
        + [pl.BlockSpec(adapters.shape, lambda i: (0, 0, 0))],
        out_specs=pl.BlockSpec((devices // steps, PACK, 128), lambda i: (i, 0, 0)),
        scratch_shapes=[pltpu.VMEM((slots, PACK, 128), BF16)],
        compiler_params=pltpu.CompilerParams(vmem_limit_bytes=VMEM_LIMIT),
        cost_estimate=pl.CostEstimate(flops=0, bytes_accessed=6 * 2**20, transcendentals=0),
        name="pick",
    )(pos, home, read, adapters)


def lora_kernel(scale, pos_ref, read_ref, rows_ref, recv_ref, last_ref, tok_ref, cot_ref,
                send_ref, down_ref, low_ref, lg_ref, mask, lgt, low_acc, grad):
    j = pl.program_id(0)
    steps = pl.num_programs(0) - 1
    width = tok_ref.shape[1]
    reads = read_ref.shape[1]
    hidden = steps * width

    def assemble(block_ref, p):
        base = pl.multiple_of(p * PAIR, 128)
        for k in range(reads):
            even, odd = block_ref[k, 0], block_ref[k, 1]
            tiles = [even[16 * t : 16 * t + 16] for t in range(4)]
            tiles += [middle_tile(even, odd)]
            tiles += [odd[16 * t : 16 * t + 16] for t in range(4)]
            for t in range(9):
                down_ref[RANK * k : RANK * k + RANK, pl.ds(base + 128 * t, 128)] = tiles[t]

    @pl.when(j == 0)
    def _():
        assemble(last_ref, steps - 1)
        device = pos_ref[0] * 16 + pos_ref[1]
        owner = lax.broadcasted_iota(jnp.int32, mask.shape, 0) // RANK
        wanted = jnp.zeros(mask.shape, jnp.int32)
        for k in range(reads):
            wanted = jnp.where(owner == k, read_ref[device, k], wanted)
        mask[...] = (wanted == rows_ref[...]).astype(F32)
        up = down_ref[:, hidden:]
        grad_t = scale * lax.dot_general(up, cot_ref[...], NT, preferred_element_type=F32) * mask[...]
        lgt[...] = grad_t.astype(BF16)
        lg_ref[...] = grad_t.T.astype(BF16)
        low_acc[...] = jnp.zeros_like(low_acc)

    @pl.when(j < steps)
    def _():
        assemble(recv_ref, j)
        at = pl.multiple_of(j * width, 128)
        low_acc[...] += lax.dot_general(
            tok_ref[...], down_ref[:, pl.ds(at, width)], NT, preferred_element_type=F32
        )
        grad[:, pl.ds(at, width)] = lax.dot_general(
            lgt[...], tok_ref[...], NN, preferred_element_type=F32
        )

    @pl.when(j == steps)
    def _():
        low = (low_acc[...] * mask[...].T).astype(BF16)
        low_ref[...] = low
        grad[:, hidden:] = scale * lax.dot_general(low, cot_ref[...], TN, preferred_element_type=F32)

    @pl.when(j > 0)
    def _():
        base = pl.multiple_of((j - 1) * PAIR, 128)
        below = lane_below(64)
        for k in range(reads):
            tiles = [grad[RANK * k : RANK * k + RANK, pl.ds(base + 128 * t, 128)] for t in range(9)]
            low, high = tiles[4][0:8], pltpu.roll(tiles[4][8:16], 64, 1)
            send_ref[k, 0] = jnp.concatenate(tiles[:4] + [jnp.where(below, low, high)], axis=0).astype(BF16)
            send_ref[k, 1] = jnp.concatenate(tiles[5:] + [jnp.where(below, high, low)], axis=0).astype(BF16)


def lora(scale, pos, read, rows, recv, tokens, cotangent):
    n, hidden = tokens.shape
    kv = cotangent.shape[1]
    reads = read.shape[1]
    ranks = reads * RANK
    shards = (hidden + kv) // SECTION
    steps = shards // 2
    width = hidden // steps
    recv = recv.reshape(reads, shards, PACK, 128)
    block = (reads, 2, PACK, 128)
    last = steps - 1
    smem = pl.BlockSpec(memory_space=pltpu.SMEM)
    return pl.pallas_call(
        functools.partial(lora_kernel, scale),
        grid=(steps + 1,),
        out_shape=(
            jax.ShapeDtypeStruct(recv.shape, BF16),
            jax.ShapeDtypeStruct((ranks, hidden + kv), BF16),
            jax.ShapeDtypeStruct((n, ranks), BF16),
            jax.ShapeDtypeStruct((n, ranks), BF16),
        ),
        in_specs=[
            smem,
            smem,
            pl.BlockSpec((1, n), lambda j: (0, 0)),
            pl.BlockSpec(block, lambda j: (0, jnp.minimum(j, last), 0, 0)),
            pl.BlockSpec(block, lambda j: (0, last, 0, 0)),
            pl.BlockSpec((n, width), lambda j: (0, jnp.minimum(j, last))),
            pl.BlockSpec((n, kv), lambda j: (0, 0)),
        ],
        out_specs=(
            pl.BlockSpec(block, lambda j: (0, jnp.maximum(j - 1, 0), 0, 0)),
            pl.BlockSpec((ranks, hidden + kv), lambda j: (0, 0)),
            pl.BlockSpec((n, ranks), lambda j: (0, 0)),
            pl.BlockSpec((n, ranks), lambda j: (0, 0)),
        ),
        scratch_shapes=[
            pltpu.VMEM((ranks, n), F32),
            pltpu.VMEM((ranks, n), BF16),
            pltpu.VMEM((n, ranks), F32),
            pltpu.VMEM((ranks, hidden + kv), F32),
        ],
        compiler_params=pltpu.CompilerParams(vmem_limit_bytes=VMEM_LIMIT),
        cost_estimate=pl.CostEstimate(flops=2**32, bytes_accessed=16 * 2**20, transcendentals=0),
        name="lora",
    )(pos, read, rows, recv, recv, tokens, cotangent)


def adam_kernel(pos_ref, home_ref, read_ref, recv_ref, a_ref, m_ref, v_ref,
                send_ref, new_a_ref, new_m_ref, new_v_ref, acc, packed):
    step = pl.program_id(0)
    tenant, odd = pos_ref[0], (pos_ref[1] & 1) == 1
    devices = recv_ref.shape[0]
    here = a_ref.shape[0]

    @pl.when(step == 0)
    def _():
        acc[...] = jnp.zeros_like(acc)

        def add(d, _):
            acc[slot_of(home_ref, read_ref, d, tenant)] += recv_ref[d].astype(F32)
            return 0

        lax.fori_loop(0, devices, add, 0, unroll=8)

    for i in range(here):
        h = step * here + i
        g = unpack_slice(acc[h], odd)
        m, v, a = (load_tiles(r, i) for r in (m_ref, v_ref, a_ref))
        m = [beta_first * m[j] + (1.0 - beta_first) * g[j] for j in range(5)]
        v = [beta_second * v[j] + (1.0 - beta_second) * g[j] * g[j] for j in range(5)]
        a = [
            a[j]
            - learn_rate * (m[j] / corr_first) / (jnp.sqrt(v[j] / corr_second) + adam_eps)
            for j in range(5)
        ]
        store_tiles(new_m_ref, i, m)
        store_tiles(new_v_ref, i, v)
        store_tiles(new_a_ref, i, a)
        packed[h] = pack_slice(a, odd).astype(BF16)

    @pl.when(step == pl.num_programs(0) - 1)
    def _():
        def copy(d, _):
            send_ref[d] = packed[slot_of(home_ref, read_ref, d, tenant)]
            return 0

        lax.fori_loop(0, devices, copy, 0, unroll=8)


def adam(pos, home, read, recv, adapters, first, second):
    slots = adapters.shape[0]
    steps = 4
    smem = pl.BlockSpec(memory_space=pltpu.SMEM)
    whole = pl.BlockSpec(recv.shape, lambda i: (0, 0, 0))
    part = pl.BlockSpec((slots // steps,) + adapters.shape[1:], lambda i: (i, 0, 0))
    stored = jax.ShapeDtypeStruct(adapters.shape, F32)
    return pl.pallas_call(
        adam_kernel,
        grid=(steps,),
        out_shape=(jax.ShapeDtypeStruct(recv.shape, BF16), stored, stored, stored),
        in_specs=[smem, smem, smem, whole, part, part, part],
        out_specs=(whole, part, part, part),
        scratch_shapes=[
            pltpu.VMEM((slots, PACK, 128), F32),
            pltpu.VMEM((slots, PACK, 128), BF16),
        ],
        compiler_params=pltpu.CompilerParams(vmem_limit_bytes=VMEM_LIMIT),
        cost_estimate=pl.CostEstimate(flops=2**24, bytes_accessed=20 * 2**20, transcendentals=0),
        name="adam",
    )(pos, home, read, recv, adapters, first, second)


def refresh_kernel(recv_ref, out_ref):
    for k in range(recv_ref.shape[0]):
        for p in range(recv_ref.shape[1] // 2):
            even, odd = recv_ref[k, 2 * p], recv_ref[k, 2 * p + 1]
            tiles = [even[16 * t : 16 * t + 16] for t in range(4)]
            tiles += [middle_tile(even, odd)]
            tiles += [odd[16 * t : 16 * t + 16] for t in range(4)]
            for t in range(9):
                out_ref[k, :, PAIR * p + 128 * t : PAIR * p + 128 * t + 128] = tiles[t]


def refresh(recv, reads):
    shards = recv.shape[0] // reads
    recv = recv.reshape(reads, shards, PACK, 128)
    return pl.pallas_call(
        refresh_kernel,
        grid=(reads // 4,),
        out_shape=jax.ShapeDtypeStruct((reads, RANK, shards * SECTION), BF16),
        in_specs=[pl.BlockSpec((4, shards, PACK, 128), lambda k: (k, 0, 0, 0))],
        out_specs=pl.BlockSpec((4, RANK, shards * SECTION), lambda k: (k, 0, 0)),
        compiler_params=pltpu.CompilerParams(vmem_limit_bytes=VMEM_LIMIT),
        cost_estimate=pl.CostEstimate(flops=0, bytes_accessed=5 * 2**20, transcendentals=0),
        name="refresh",
    )(recv)


def base_kernel(scale, final, half_ref, w_ref, *rest):
    toks, downs, rest = rest[:4], rest[4:8], rest[8:]
    cot_ref, up_ref, low_ref, lg_ref, *rest = rest
    if final:
        part_ref, _, tg_ref, values_ref, row, down, acc, out, sems = rest
    else:
        tg_ref, values_ref, row, down, acc, out, sems = rest
    i = pl.program_id(0)
    steps = pl.num_programs(0)
    cols = row.shape[1] // 4
    slot = lax.rem(i, 2)

    def copies(step, at):
        for t in range(4):
            start = pl.multiple_of((2 * (4 * step + t) + half_ref[0]) * cols, cols)
            yield pltpu.make_async_copy(out.at[at, t], tg_ref.at[:, pl.ds(start, cols)], sems.at[at, t])

    @pl.when(i == 0)
    def _():
        if final:
            acc[...] = part_ref[...]
        else:
            acc[...] = scale * jnp.dot(low_ref[...], up_ref[...], preferred_element_type=F32)

    @pl.when(i >= 2)
    def _():
        for copy in copies(i - 2, slot):
            copy.wait()

    for t in range(4):
        row[:, cols * t : cols * t + cols] = toks[t][...]
        down[:, cols * t : cols * t + cols] = downs[t][...]
    acc[...] += jnp.dot(row[...], w_ref[...], preferred_element_type=F32)
    grad = lax.dot_general(cot_ref[...], w_ref[...], NT, preferred_element_type=F32) + jnp.dot(
        lg_ref[...], down[...], preferred_element_type=F32
    )
    for t in range(4):
        out[slot, t] = grad[:, cols * t : cols * t + cols].astype(BF16)
    for copy in copies(i, slot):
        copy.start()

    @pl.when(i == steps - 1)
    def _():
        values_ref[...] = acc[...].astype(values_ref.dtype)
        for copy in copies(i - 1, 1 - slot):
            copy.wait()
        for copy in copies(i, slot):
            copy.wait()


def base(scale, half, w_half, tokens, cotangent, down, low, lg, part=None, grad=None):
    final = part is not None
    n, hidden = tokens.shape
    kv = cotangent.shape[1]
    ranks = low.shape[1]
    rows = 256
    steps = w_half.shape[0] // (4 * rows)
    in_specs = [pl.BlockSpec((4 * rows, kv), lambda i, h: (i, 0))]
    for height in (n, ranks):
        for t in range(4):
            in_specs.append(
                pl.BlockSpec((height, rows), lambda i, h, t=t: (0, 2 * (4 * i + t) + h[0]))
            )
    in_specs += [
        pl.BlockSpec((n, kv), lambda i, h: (0, 0)),
        pl.BlockSpec((ranks, kv), lambda i, h: (0, hidden // kv)),
        pl.BlockSpec((n, ranks), lambda i, h: (0, 0)),
        pl.BlockSpec((n, ranks), lambda i, h: (0, 0)),
    ]
    args = [half, w_half] + [tokens] * 4 + [down] * 4 + [cotangent, down, low, lg]
    aliases = {}
    if final:
        in_specs += [pl.BlockSpec((n, kv), lambda i, h: (0, 0)), pl.BlockSpec(memory_space=pl.ANY)]
        args += [part, grad]
        aliases = {len(args) - 1: 0}
    return pl.pallas_call(
        functools.partial(base_kernel, scale, final),
        grid_spec=pltpu.PrefetchScalarGridSpec(
            num_scalar_prefetch=1,
            grid=(steps,),
            in_specs=in_specs,
            out_specs=(
                pl.BlockSpec(memory_space=pl.ANY),
                pl.BlockSpec((n, kv), lambda i, h: (0, 0)),
            ),
            scratch_shapes=[
                pltpu.VMEM((n, 4 * rows), BF16),
                pltpu.VMEM((ranks, 4 * rows), BF16),
                pltpu.VMEM((n, kv), F32),
                pltpu.VMEM((2, 4, n, rows), BF16),
                pltpu.SemaphoreType.DMA((2, 4)),
            ],
        ),
        out_shape=(
            jax.ShapeDtypeStruct((n, hidden), BF16),
            jax.ShapeDtypeStruct((n, kv), BF16 if final else F32),
        ),
        input_output_aliases=aliases,
        compiler_params=pltpu.CompilerParams(vmem_limit_bytes=VMEM_LIMIT),
        cost_estimate=pl.CostEstimate(flops=9 * 2**30, bytes_accessed=20 * 2**20, transcendentals=0),
        name="base_final" if final else "base_first",
    )(*args)


def exchange(blocks):
    return lax.all_to_all(blocks, ("x", "core", "fsdp"), split_axis=0, concat_axis=0, tiled=True)


def per_device(
    tokens,
    cotangent,
    value_weight,
    adapters,
    first_moment,
    second_moment,
    tenant_home,
    read_tenants,
    row_tenant,
):
    hidden = tokens.shape[1]
    reads = read_tenants.shape[1]
    core = lax.axis_index("core").astype(jnp.int32)
    tenant = 2 * lax.axis_index("x").astype(jnp.int32) + core
    pos = jnp.stack([tenant, lax.axis_index("fsdp").astype(jnp.int32)])
    scale = 2.0 / math.sqrt(hidden * RANK)

    half_rows = value_weight.shape[0] // 2
    mine = lax.dynamic_slice_in_dim(value_weight, core * half_rows, half_rows, 0)
    w_mine = lax.all_gather(mine, "fsdp", axis=0, tiled=True)

    fetched = exchange(pick(pos, tenant_home, read_tenants, adapters))
    send, down, low, lg = lora(
        scale, pos, read_tenants, row_tenant.reshape(1, -1), fetched, tokens, cotangent
    )
    received = exchange(send.reshape(fetched.shape))
    fresh, new_adapters, new_first, new_second = adam(
        pos, tenant_home, read_tenants, received, adapters, first_moment, second_moment
    )
    w_mine, fresh = lax.optimization_barrier((w_mine, fresh))
    w_other = lax.ppermute(w_mine, "core", [(0, 1), (1, 0)])
    renewed = exchange(fresh)
    grad, part = base(scale, core[None], w_mine, tokens, cotangent, down, low, lg)
    token_grad, values = base(
        scale, 1 - core[None], w_other, tokens, cotangent, down, low, lg, part, grad
    )
    values, renewed = lax.optimization_barrier((values, renewed))
    refreshed = refresh(renewed, reads)
    return (values, token_grad, new_adapters, new_first, new_second, refreshed)


def solution(mesh):
    shape = mesh.devices.shape
    inner = Mesh(mesh.devices.reshape(shape[0] // 2, 2, shape[1]), ("x", "core", "fsdp"))
    rows = ("x", "core", "fsdp")
    tenant = ("x", "core")
    return jax.shard_map(
        per_device,
        mesh=inner,
        in_specs=(
            P(rows, None),
            P(rows, None),
            P("fsdp", None),
            P(tenant, None, "fsdp"),
            P(tenant, None, "fsdp"),
            P(tenant, None, "fsdp"),
            P(),
            P(),
            P(rows),
        ),
        out_specs=(
            P(rows, None),
            P(rows, None),
            P(tenant, None, "fsdp"),
            P(tenant, None, "fsdp"),
            P(tenant, None, "fsdp"),
            P(rows, None, None),
        ),
        check_vma=False,
    )
```

```python
import functools
import math

import jax
import jax.numpy as jnp
from jax import lax
from jax.experimental import pallas as pl
from jax.experimental.pallas import tpu as pltpu
from jax.sharding import Mesh, PartitionSpec as P

beta_first = 0.9
beta_second = 0.95
learn_rate = 0.1
adam_eps = 1e-08
corr_first = 1.0 - 0.9**10
corr_second = 1.0 - 0.95**10

BF16 = jnp.bfloat16
F32 = jnp.float32
NT = (((1,), (1,)), ((), ()))
NN = (((1,), (0,)), ((), ()))
TN = (((0,), (0,)), ((), ()))
MIB = 2**20
RANK = 16
SECTION = 576
PACK = 72
PAIR = 2 * SECTION
LORA_STEPS = 4


def lane_below(half):
    return lax.broadcasted_iota(jnp.int32, (8, 128), 1) < half


def halves(low, high):
    return jnp.where(lax.broadcasted_iota(jnp.int32, low.shape, 1) < 64, low, high)


def pack_slice(tiles, odd):
    rolled = [pltpu.roll(t, 64, 1) for t in tiles]
    body = [jnp.where(odd, halves(rolled[j], rolled[j + 1]), tiles[j]) for j in range(4)]
    tail = jnp.where(
        odd,
        halves(tiles[0][8:16], rolled[0][0:8]),
        halves(tiles[4][0:8], rolled[4][8:16]),
    )
    return jnp.concatenate(body + [tail], axis=0)


def unpack_slice(block, odd):
    tail = block[64:72]
    tail_rolled = pltpu.roll(tail, 64, 1)
    tiles = [block[16 * j : 16 * j + 16] for j in range(4)]
    rolled = [pltpu.roll(t, 64, 1) for t in tiles]
    last = jnp.concatenate([tail, tail_rolled], axis=0)
    before = jnp.concatenate([tail_rolled, tail], axis=0)
    row = [jnp.where(odd, halves(before, rolled[0]), tiles[0])]
    row += [jnp.where(odd, halves(rolled[j - 1], rolled[j]), tiles[j]) for j in range(1, 4)]
    return row + [jnp.where(odd, rolled[3], last)]


def load_tiles(ref, h):
    tail = jnp.concatenate([ref[h, :, 512:SECTION], jnp.zeros((RANK, 640 - SECTION), F32)], axis=1)
    return [ref[h, :, 128 * j : 128 * j + 128] for j in range(4)] + [tail]


def store_tiles(ref, h, tiles):
    for j in range(4):
        ref[h, :, 128 * j : 128 * j + 128] = tiles[j]
    ref[h, :, 512:SECTION] = tiles[4][:, : SECTION - 512]


def middle_tile(even, odd):
    te, to = even.astype(F32)[64:72], odd.astype(F32)[64:72]
    below = lane_below(64)
    low = jnp.where(below, te, to)
    high = pltpu.roll(jnp.where(below, to, te), 64, 1)
    return jnp.concatenate([low, high], axis=0).astype(BF16)


def slot_of(home_ref, read_ref, d, tenant):
    return home_ref[read_ref[tenant, d]] - RANK * tenant


def pick_kernel(pos_ref, home_ref, read_ref, adapters_ref, out_ref, packed):
    step = pl.program_id(0)
    tenant, odd = pos_ref[0], (pos_ref[1] & 1) == 1
    slots, here = adapters_ref.shape[0], out_ref.shape[0]

    @pl.when(step == 0)
    def _():
        def fill(h, _):
            packed[h] = pack_slice(load_tiles(adapters_ref, h), odd).astype(BF16)
            return 0

        lax.fori_loop(0, slots, fill, 0, unroll=2)

    def copy(d, _):
        out_ref[d] = packed[slot_of(home_ref, read_ref, step * here + d, tenant)]
        return 0

    lax.fori_loop(0, here, copy, 0, unroll=8)


def pick(pos, home, read, adapters):
    slots, devices = adapters.shape[0], read.shape[1]
    steps = 2
    return pl.pallas_call(
        pick_kernel,
        grid=(steps,),
        out_shape=jax.ShapeDtypeStruct((devices, PACK, 128), BF16),
        in_specs=[pl.BlockSpec(memory_space=pltpu.SMEM)] * 3
        + [pl.BlockSpec(adapters.shape, lambda i: (0, 0, 0))],
        out_specs=pl.BlockSpec((devices // steps, PACK, 128), lambda i: (i, 0, 0)),
        scratch_shapes=[pltpu.VMEM((slots, PACK, 128), BF16)],
        compiler_params=pltpu.CompilerParams(vmem_limit_bytes=56 * MIB),
        cost_estimate=pl.CostEstimate(flops=0, bytes_accessed=6 * 2**20, transcendentals=0),
        name="pick",
    )(pos, home, read, adapters)


def lora_kernel(scale, pos_ref, read_ref, rows_ref, recv_ref, last_ref, tok_ref, cot_ref,
                send_ref, down_ref, low_ref, lg_ref, adapter, mask, lgt, low_acc, grad, sems):
    j = pl.program_id(0)
    steps = pl.num_programs(0) - 1
    width = tok_ref.shape[1]
    reads = read_ref.shape[0]
    pairs = recv_ref.shape[1] // 2
    part = pairs * PAIR
    hidden = steps * width

    def assemble(block_ref, p):
        for q in range(pairs):
            base = pl.multiple_of(p * part + q * PAIR, 128)
            for k in range(reads):
                even, odd = block_ref[k, 2 * q], block_ref[k, 2 * q + 1]
                tiles = [even[16 * t : 16 * t + 16] for t in range(4)]
                tiles += [middle_tile(even, odd)]
                tiles += [odd[16 * t : 16 * t + 16] for t in range(4)]
                for t in range(9):
                    adapter[RANK * k : RANK * k + RANK, pl.ds(base + 128 * t, 128)] = tiles[t]

    def keep(p):
        at = pl.ds(pl.multiple_of(p * part, 128), part)
        return pltpu.make_async_copy(adapter.at[:, at], down_ref.at[:, at], sems.at[p])

    @pl.when(j == 0)
    def _():
        assemble(last_ref, steps - 1)
        keep(steps - 1).start()
        device = pos_ref[0] * 16 + pos_ref[1]
        owner = lax.broadcasted_iota(jnp.int32, mask.shape, 0) // RANK
        wanted = jnp.zeros(mask.shape, jnp.int32)
        for k in range(reads):
            wanted = jnp.where(owner == k, read_ref[k, device], wanted)
        mask[...] = (wanted == rows_ref[...]).astype(F32)
        up = adapter[:, hidden:]
        grad_t = scale * lax.dot_general(up, cot_ref[...], NT, preferred_element_type=F32) * mask[...]
        lgt[...] = grad_t.astype(BF16)
        lg_ref[...] = grad_t.T.astype(BF16)
        low_acc[...] = jnp.zeros_like(low_acc)

    @pl.when(j < steps - 1)
    def _():
        assemble(recv_ref, j)
        keep(j).start()

    @pl.when(j < steps)
    def _():
        at = pl.ds(pl.multiple_of(j * width, 128), width)
        low_acc[...] += lax.dot_general(adapter[:, at], tok_ref[...], NT, preferred_element_type=F32)
        grad[:, at] = lax.dot_general(lgt[...], tok_ref[...], NN, preferred_element_type=F32)

    @pl.when(j == steps)
    def _():
        low_t = low_acc[...] * mask[...]
        low_ref[...] = low_t.T.astype(BF16)
        grad[:, hidden:] = scale * lax.dot_general(
            low_t.astype(BF16), cot_ref[...], NN, preferred_element_type=F32
        )

    @pl.when(j > 0)
    def _():
        below = lane_below(64)
        for q in range(pairs):
            base = pl.multiple_of((j - 1) * part + q * PAIR, 128)
            for k in range(reads):
                rows = slice(RANK * k, RANK * k + RANK)
                tiles = [grad[rows, pl.ds(base + 128 * t, 128)] for t in range(9)]
                low, high = tiles[4][0:8], pltpu.roll(tiles[4][8:16], 64, 1)
                first, second = jnp.where(below, low, high), jnp.where(below, high, low)
                send_ref[k, 2 * q] = jnp.concatenate(tiles[:4] + [first], axis=0).astype(BF16)
                send_ref[k, 2 * q + 1] = jnp.concatenate(tiles[5:] + [second], axis=0).astype(BF16)

    @pl.when(j == steps)
    def _():
        for p in range(adapter.shape[1] // part):
            keep(p).wait()


def lora(scale, pos, read, rows, recv, tokens, cotangent):
    n, hidden = tokens.shape
    kv = cotangent.shape[1]
    reads = read.shape[0]
    ranks = reads * RANK
    shards = (hidden + kv) // SECTION
    steps = LORA_STEPS
    width = hidden // steps
    recv = recv.reshape(reads, shards, PACK, 128)
    block = (reads, shards // steps, PACK, 128)
    last = steps - 1
    smem = pl.BlockSpec(memory_space=pltpu.SMEM)
    return pl.pallas_call(
        functools.partial(lora_kernel, scale),
        grid=(steps + 1,),
        out_shape=(
            jax.ShapeDtypeStruct(recv.shape, BF16),
            jax.ShapeDtypeStruct((ranks, hidden + kv), BF16),
            jax.ShapeDtypeStruct((n, ranks), BF16),
            jax.ShapeDtypeStruct((n, ranks), BF16),
        ),
        in_specs=[
            smem,
            smem,
            pl.BlockSpec((1, n), lambda j: (0, 0)),
            pl.BlockSpec(block, lambda j: (0, jnp.minimum(j, last - 1), 0, 0)),
            pl.BlockSpec(block, lambda j: (0, last, 0, 0)),
            pl.BlockSpec((n, width), lambda j: (0, jnp.minimum(j, last))),
            pl.BlockSpec((n, kv), lambda j: (0, 0)),
        ],
        out_specs=(
            pl.BlockSpec(block, lambda j: (0, jnp.maximum(j - 1, 0), 0, 0)),
            pl.BlockSpec(memory_space=pl.ANY),
            pl.BlockSpec((n, ranks), lambda j: (0, 0)),
            pl.BlockSpec((n, ranks), lambda j: (0, 0)),
        ),
        scratch_shapes=[
            pltpu.VMEM((ranks, hidden + kv), BF16),
            pltpu.VMEM((ranks, n), F32),
            pltpu.VMEM((ranks, n), BF16),
            pltpu.VMEM((ranks, n), F32),
            pltpu.VMEM((ranks, hidden + kv), F32),
            pltpu.SemaphoreType.DMA((steps,)),
        ],
        compiler_params=pltpu.CompilerParams(vmem_limit_bytes=56 * MIB),
        cost_estimate=pl.CostEstimate(flops=2**32, bytes_accessed=16 * 2**20, transcendentals=0),
        name="lora",
    )(pos, read, rows, recv, recv, tokens, cotangent)


def adam_kernel(pos_ref, home_ref, read_ref, recv_ref, a_ref, m_ref, v_ref,
                send_ref, new_a_ref, new_m_ref, new_v_ref, acc, packed):
    step = pl.program_id(0)
    tenant, odd = pos_ref[0], (pos_ref[1] & 1) == 1
    devices = recv_ref.shape[0]
    here = a_ref.shape[0]

    @pl.when(step == 0)
    def _():
        acc[...] = jnp.zeros_like(acc)

        def add(d, _):
            acc[slot_of(home_ref, read_ref, d, tenant)] += recv_ref[d].astype(F32)
            return 0

        lax.fori_loop(0, devices, add, 0, unroll=8)

    for i in range(here):
        h = step * here + i
        g = unpack_slice(acc[h], odd)
        m, v, a = (load_tiles(r, i) for r in (m_ref, v_ref, a_ref))
        m = [beta_first * m[j] + (1.0 - beta_first) * g[j] for j in range(5)]
        v = [beta_second * v[j] + (1.0 - beta_second) * g[j] * g[j] for j in range(5)]
        a = [
            a[j]
            - learn_rate * (m[j] / corr_first) / (jnp.sqrt(v[j] / corr_second) + adam_eps)
            for j in range(5)
        ]
        store_tiles(new_m_ref, i, m)
        store_tiles(new_v_ref, i, v)
        store_tiles(new_a_ref, i, a)
        packed[h] = pack_slice(a, odd).astype(BF16)

    @pl.when(step == pl.num_programs(0) - 1)
    def _():
        def copy(d, _):
            send_ref[d] = packed[slot_of(home_ref, read_ref, d, tenant)]
            return 0

        lax.fori_loop(0, devices, copy, 0, unroll=8)


def adam(pos, home, read, recv, adapters, first, second):
    slots = adapters.shape[0]
    steps = 4
    smem = pl.BlockSpec(memory_space=pltpu.SMEM)
    whole = pl.BlockSpec(recv.shape, lambda i: (0, 0, 0))
    part = pl.BlockSpec((slots // steps,) + adapters.shape[1:], lambda i: (i, 0, 0))
    stored = jax.ShapeDtypeStruct(adapters.shape, F32)
    return pl.pallas_call(
        adam_kernel,
        grid=(steps,),
        out_shape=(jax.ShapeDtypeStruct(recv.shape, BF16), stored, stored, stored),
        in_specs=[smem, smem, smem, whole, part, part, part],
        out_specs=(whole, part, part, part),
        scratch_shapes=[
            pltpu.VMEM((slots, PACK, 128), F32),
            pltpu.VMEM((slots, PACK, 128), BF16),
        ],
        compiler_params=pltpu.CompilerParams(vmem_limit_bytes=32 * MIB),
        cost_estimate=pl.CostEstimate(flops=2**24, bytes_accessed=20 * 2**20, transcendentals=0),
        name="adam",
    )(pos, home, read, recv, adapters, first, second)


def refresh_kernel(recv_ref, out_ref):
    for k in range(recv_ref.shape[0]):
        for p in range(recv_ref.shape[1] // 2):
            even, odd = recv_ref[k, 2 * p], recv_ref[k, 2 * p + 1]
            tiles = [even[16 * t : 16 * t + 16] for t in range(4)]
            tiles += [middle_tile(even, odd)]
            tiles += [odd[16 * t : 16 * t + 16] for t in range(4)]
            for t in range(9):
                out_ref[k, :, PAIR * p + 128 * t : PAIR * p + 128 * t + 128] = tiles[t]


def refresh(recv, reads):
    shards = recv.shape[0] // reads
    recv = recv.reshape(reads, shards, PACK, 128)
    return pl.pallas_call(
        refresh_kernel,
        grid=(reads // 4,),
        out_shape=jax.ShapeDtypeStruct((reads, RANK, shards * SECTION), BF16),
        in_specs=[pl.BlockSpec((4, shards, PACK, 128), lambda k: (k, 0, 0, 0))],
        out_specs=pl.BlockSpec((4, RANK, shards * SECTION), lambda k: (k, 0, 0)),
        compiler_params=pltpu.CompilerParams(vmem_limit_bytes=16 * MIB),
        cost_estimate=pl.CostEstimate(flops=0, bytes_accessed=5 * 2**20, transcendentals=0),
        name="refresh",
    )(recv)


def base_kernel(scale, final, half_ref, w_ref, *rest):
    toks, downs, rest = rest[:4], rest[4:8], rest[8:]
    cot_ref, up_ref, low_ref, lg_ref, *rest = rest
    if final:
        part_ref, _, tg_ref, values_ref, row, down, acc, out, sems = rest
    else:
        tg_ref, values_ref, row, down, acc, out, sems = rest
    i = pl.program_id(0)
    steps = pl.num_programs(0)
    cols = row.shape[1] // 4
    slot = lax.rem(i, 2)

    def copies(step, at):
        for t in range(4):
            start = pl.multiple_of((2 * (4 * step + t) + half_ref[0]) * cols, cols)
            yield pltpu.make_async_copy(out.at[at, t], tg_ref.at[:, pl.ds(start, cols)], sems.at[at, t])

    @pl.when(i == 0)
    def _():
        if final:
            acc[...] = part_ref[...]
        else:
            acc[...] = scale * jnp.dot(low_ref[...], up_ref[...], preferred_element_type=F32)

    @pl.when(i >= 2)
    def _():
        for copy in copies(i - 2, slot):
            copy.wait()

    for t in range(4):
        row[:, cols * t : cols * t + cols] = toks[t][...]
        down[:, cols * t : cols * t + cols] = downs[t][...]
    acc[...] += jnp.dot(row[...], w_ref[...], preferred_element_type=F32)
    grad = lax.dot_general(cot_ref[...], w_ref[...], NT, preferred_element_type=F32) + jnp.dot(
        lg_ref[...], down[...], preferred_element_type=F32
    )
    for t in range(4):
        out[slot, t] = grad[:, cols * t : cols * t + cols].astype(BF16)
    for copy in copies(i, slot):
        copy.start()

    @pl.when(i == steps - 1)
    def _():
        values_ref[...] = acc[...].astype(values_ref.dtype)
        for copy in copies(i - 1, 1 - slot):
            copy.wait()
        for copy in copies(i, slot):
            copy.wait()


def base(scale, half, w_half, tokens, cotangent, down, low, lg, part=None, grad=None):
    final = part is not None
    n, hidden = tokens.shape
    kv = cotangent.shape[1]
    ranks = low.shape[1]
    rows = 256
    steps = w_half.shape[0] // (4 * rows)
    in_specs = [pl.BlockSpec((4 * rows, kv), lambda i, h: (i, 0))]
    for height in (n, ranks):
        for t in range(4):
            in_specs.append(
                pl.BlockSpec((height, rows), lambda i, h, t=t: (0, 2 * (4 * i + t) + h[0]))
            )
    in_specs += [
        pl.BlockSpec((n, kv), lambda i, h: (0, 0)),
        pl.BlockSpec((ranks, kv), lambda i, h: (0, hidden // kv)),
        pl.BlockSpec((n, ranks), lambda i, h: (0, 0)),
        pl.BlockSpec((n, ranks), lambda i, h: (0, 0)),
    ]
    args = [half, w_half] + [tokens] * 4 + [down] * 4 + [cotangent, down, low, lg]
    aliases = {}
    if final:
        in_specs += [pl.BlockSpec((n, kv), lambda i, h: (0, 0)), pl.BlockSpec(memory_space=pl.ANY)]
        args += [part, grad]
        aliases = {len(args) - 1: 0}
    return pl.pallas_call(
        functools.partial(base_kernel, scale, final),
        grid_spec=pltpu.PrefetchScalarGridSpec(
            num_scalar_prefetch=1,
            grid=(steps,),
            in_specs=in_specs,
            out_specs=(
                pl.BlockSpec(memory_space=pl.ANY),
                pl.BlockSpec((n, kv), lambda i, h: (0, 0)),
            ),
            scratch_shapes=[
                pltpu.VMEM((n, 4 * rows), BF16),
                pltpu.VMEM((ranks, 4 * rows), BF16),
                pltpu.VMEM((n, kv), F32),
                pltpu.VMEM((2, 4, n, rows), BF16),
                pltpu.SemaphoreType.DMA((2, 4)),
            ],
        ),
        out_shape=(
            jax.ShapeDtypeStruct((n, hidden), BF16),
            jax.ShapeDtypeStruct((n, kv), BF16 if final else F32),
        ),
        input_output_aliases=aliases,
        compiler_params=pltpu.CompilerParams(vmem_limit_bytes=56 * MIB),
        cost_estimate=pl.CostEstimate(flops=9 * 2**30, bytes_accessed=20 * 2**20, transcendentals=0),
        name="base_final" if final else "base_first",
    )(*args)


def exchange(blocks):
    return lax.all_to_all(blocks, ("x", "core", "y", "z"), split_axis=0, concat_axis=0, tiled=True)


def per_device(
    tokens,
    cotangent,
    value_weight,
    adapters,
    first_moment,
    second_moment,
    tenant_home,
    read_tenants,
    row_tenant,
):
    hidden = tokens.shape[1]
    read_tenants = read_tenants.T
    reads = read_tenants.shape[0]
    core = lax.axis_index("core").astype(jnp.int32)
    shard = lax.axis_index(("y", "z")).astype(jnp.int32)
    pos = jnp.stack([2 * lax.axis_index("x").astype(jnp.int32) + core, shard])
    scale = 2.0 / math.sqrt(hidden * RANK)

    half = value_weight.shape[0] // 2
    mine = lax.dynamic_slice_in_dim(value_weight, core * half, half, 0)
    w_mine = lax.all_gather(mine, ("y", "z"), axis=0, tiled=True)

    fetched = exchange(pick(pos, tenant_home, read_tenants, adapters))
    send, down, low, lg = lora(
        scale, pos, read_tenants, row_tenant.reshape(1, -1), fetched, tokens, cotangent
    )
    received = exchange(send.reshape(fetched.shape))
    fresh, new_adapters, new_first, new_second = adam(
        pos, tenant_home, read_tenants, received, adapters, first_moment, second_moment
    )
    w_mine, fresh = lax.optimization_barrier((w_mine, fresh))
    w_other = lax.ppermute(w_mine, "core", [(0, 1), (1, 0)])
    renewed = exchange(fresh)
    grad, part = base(scale, core[None], w_mine, tokens, cotangent, down, low, lg)
    token_grad, values = base(
        scale, 1 - core[None], w_other, tokens, cotangent, down, low, lg, part, grad
    )
    values, renewed = lax.optimization_barrier((values, renewed))
    refreshed = refresh(renewed, reads)
    return (values, token_grad, new_adapters, new_first, new_second, refreshed)


def solution(mesh):
    shape = mesh.devices.shape
    inner = Mesh(mesh.devices.reshape(shape[0] // 2, 2, 4, 4), ("x", "core", "y", "z"))
    rows = ("x", "core", "y", "z")
    tenant, fsdp = ("x", "core"), ("y", "z")
    return jax.shard_map(
        per_device,
        mesh=inner,
        in_specs=(
            P(rows, None),
            P(rows, None),
            P(fsdp, None),
            P(tenant, None, fsdp),
            P(tenant, None, fsdp),
            P(tenant, None, fsdp),
            P(),
            P(),
            P(rows),
        ),
        out_specs=(
            P(rows, None),
            P(rows, None),
            P(tenant, None, fsdp),
            P(tenant, None, fsdp),
            P(tenant, None, fsdp),
            P(rows, None, None),
        ),
        check_vma=False,
    )
```

```python
import functools
import math

import jax
import jax.numpy as jnp
from jax import lax
from jax.experimental import pallas as pl
from jax.experimental.pallas import tpu as pltpu
from jax.sharding import Mesh, PartitionSpec as P

beta_first = 0.9
beta_second = 0.95
learn_rate = 0.1
adam_eps = 1e-08
corr_first = 1.0 - 0.9**10
corr_second = 1.0 - 0.95**10

BF16 = jnp.bfloat16
F32 = jnp.float32
NT = (((1,), (1,)), ((), ()))
NN = (((1,), (0,)), ((), ()))
TN = (((0,), (0,)), ((), ()))
MIB = 2**20
BASE_ROWS = 1024
RANK = 16
SECTION = 576
PACK = 72
PAIR = 2 * SECTION
LORA_STEPS = 8


def lane_below(half):
    return lax.broadcasted_iota(jnp.int32, (8, 128), 1) < half


def halves(low, high):
    return jnp.where(lax.broadcasted_iota(jnp.int32, low.shape, 1) < 64, low, high)


def pack_slice(tiles, odd):
    rolled = [pltpu.roll(t, 64, 1) for t in tiles]
    body = [jnp.where(odd, halves(rolled[j], rolled[j + 1]), tiles[j]) for j in range(4)]
    tail = jnp.where(
        odd,
        halves(tiles[0][8:16], rolled[0][0:8]),
        halves(tiles[4][0:8], rolled[4][8:16]),
    )
    return jnp.concatenate(body + [tail], axis=0)


def unpack_slice(block, odd):
    tail = block[64:72]
    tail_rolled = pltpu.roll(tail, 64, 1)
    tiles = [block[16 * j : 16 * j + 16] for j in range(4)]
    rolled = [pltpu.roll(t, 64, 1) for t in tiles]
    last = jnp.concatenate([tail, tail_rolled], axis=0)
    before = jnp.concatenate([tail_rolled, tail], axis=0)
    row = [jnp.where(odd, halves(before, rolled[0]), tiles[0])]
    row += [jnp.where(odd, halves(rolled[j - 1], rolled[j]), tiles[j]) for j in range(1, 4)]
    return row + [jnp.where(odd, rolled[3], last)]


def load_tiles(ref, h):
    tail = jnp.concatenate([ref[h, :, 512:SECTION], jnp.zeros((RANK, 640 - SECTION), F32)], axis=1)
    return [ref[h, :, 128 * j : 128 * j + 128] for j in range(4)] + [tail]


def store_tiles(ref, h, tiles):
    for j in range(4):
        ref[h, :, 128 * j : 128 * j + 128] = tiles[j]
    ref[h, :, 512:SECTION] = tiles[4][:, : SECTION - 512]


def middle_tile(even, odd):
    te, to = even.astype(F32)[64:72], odd.astype(F32)[64:72]
    below = lane_below(64)
    low = jnp.where(below, te, to)
    high = pltpu.roll(jnp.where(below, to, te), 64, 1)
    return jnp.concatenate([low, high], axis=0).astype(BF16)


def slot_of(home_ref, read_ref, d, tenant):
    return home_ref[read_ref[tenant, d]] - RANK * tenant


def pick_kernel(pos_ref, home_ref, read_ref, adapters_ref, out_ref, packed):
    step = pl.program_id(0)
    tenant, odd = pos_ref[0], (pos_ref[1] & 1) == 1
    slots, here = adapters_ref.shape[0], out_ref.shape[0]

    @pl.when(step == 0)
    def _():
        def fill(h, _):
            packed[h] = pack_slice(load_tiles(adapters_ref, h), odd).astype(BF16)
            return 0

        lax.fori_loop(0, slots, fill, 0, unroll=2)

    def copy(d, _):
        out_ref[d] = packed[slot_of(home_ref, read_ref, step * here + d, tenant)]
        return 0

    lax.fori_loop(0, here, copy, 0, unroll=8)


def pick(pos, home, read, adapters):
    slots, devices = adapters.shape[0], read.shape[1]
    steps = 2
    return pl.pallas_call(
        pick_kernel,
        grid=(steps,),
        out_shape=jax.ShapeDtypeStruct((devices, PACK, 128), BF16),
        in_specs=[pl.BlockSpec(memory_space=pltpu.SMEM)] * 3
        + [pl.BlockSpec(adapters.shape, lambda i: (0, 0, 0))],
        out_specs=pl.BlockSpec((devices // steps, PACK, 128), lambda i: (i, 0, 0)),
        scratch_shapes=[pltpu.VMEM((slots, PACK, 128), BF16)],
        compiler_params=pltpu.CompilerParams(vmem_limit_bytes=56 * MIB),
        cost_estimate=pl.CostEstimate(flops=0, bytes_accessed=6 * 2**20, transcendentals=0),
        name="pick",
    )(pos, home, read, adapters)


def lora_kernel(scale, pos_ref, read_ref, rows_ref, recv_ref, last_ref, tok_ref, cot_ref,
                send_ref, down_ref, low_ref, lg_ref, adapter, mask, lgt, low_acc, grad, sems):
    j = pl.program_id(0)
    steps = pl.num_programs(0) - 1
    width = tok_ref.shape[1]
    reads = read_ref.shape[0]
    pairs = recv_ref.shape[1] // 2
    part = pairs * PAIR
    hidden = steps * width

    def assemble(block_ref, p):
        for q in range(pairs):
            base = pl.multiple_of(p * part + q * PAIR, 128)
            for k in range(reads):
                even, odd = block_ref[k, 2 * q], block_ref[k, 2 * q + 1]
                tiles = [even[16 * t : 16 * t + 16] for t in range(4)]
                tiles += [middle_tile(even, odd)]
                tiles += [odd[16 * t : 16 * t + 16] for t in range(4)]
                for t in range(9):
                    adapter[RANK * k : RANK * k + RANK, pl.ds(base + 128 * t, 128)] = tiles[t]

    def keep(p):
        at = pl.ds(pl.multiple_of(p * part, 128), part)
        return pltpu.make_async_copy(adapter.at[:, at], down_ref.at[:, at], sems.at[p])

    @pl.when(j == 0)
    def _():
        assemble(last_ref, steps - 1)
        keep(steps - 1).start()
        device = pos_ref[0] * 16 + pos_ref[1]
        owner = lax.broadcasted_iota(jnp.int32, mask.shape, 0) // RANK
        wanted = jnp.zeros(mask.shape, jnp.int32)
        for k in range(reads):
            wanted = jnp.where(owner == k, read_ref[k, device], wanted)
        mask[...] = (wanted == rows_ref[...]).astype(F32)
        up = adapter[:, hidden:]
        grad_t = scale * lax.dot_general(up, cot_ref[...], NT, preferred_element_type=F32) * mask[...]
        lgt[...] = grad_t.astype(BF16)
        lg_ref[...] = grad_t.T.astype(BF16)
        low_acc[...] = jnp.zeros_like(low_acc)

    @pl.when(j < steps - 1)
    def _():
        assemble(recv_ref, j)
        keep(j).start()

    @pl.when(j < steps)
    def _():
        at = pl.ds(pl.multiple_of(j * width, 128), width)
        low_acc[...] += lax.dot_general(adapter[:, at], tok_ref[...], NT, preferred_element_type=F32)
        grad[:, at] = lax.dot_general(lgt[...], tok_ref[...], NN, preferred_element_type=F32)

    @pl.when(j == steps)
    def _():
        low_t = low_acc[...] * mask[...]
        low_ref[...] = low_t.T.astype(BF16)
        grad[:, hidden:] = scale * lax.dot_general(
            low_t.astype(BF16), cot_ref[...], NN, preferred_element_type=F32
        )

    @pl.when(j > 0)
    def _():
        below = lane_below(64)
        for q in range(pairs):
            base = pl.multiple_of((j - 1) * part + q * PAIR, 128)
            for k in range(reads):
                rows = slice(RANK * k, RANK * k + RANK)
                tiles = [grad[rows, pl.ds(base + 128 * t, 128)] for t in range(9)]
                low, high = tiles[4][0:8], pltpu.roll(tiles[4][8:16], 64, 1)
                first, second = jnp.where(below, low, high), jnp.where(below, high, low)
                send_ref[k, 2 * q] = jnp.concatenate(tiles[:4] + [first], axis=0).astype(BF16)
                send_ref[k, 2 * q + 1] = jnp.concatenate(tiles[5:] + [second], axis=0).astype(BF16)

    @pl.when(j == steps)
    def _():
        for p in range(adapter.shape[1] // part):
            keep(p).wait()


def lora(scale, pos, read, rows, recv, tokens, cotangent):
    n, hidden = tokens.shape
    kv = cotangent.shape[1]
    reads = read.shape[0]
    ranks = reads * RANK
    shards = (hidden + kv) // SECTION
    steps = LORA_STEPS
    width = hidden // steps
    recv = recv.reshape(reads, shards, PACK, 128)
    block = (reads, shards // steps, PACK, 128)
    last = steps - 1
    smem = pl.BlockSpec(memory_space=pltpu.SMEM)
    return pl.pallas_call(
        functools.partial(lora_kernel, scale),
        grid=(steps + 1,),
        out_shape=(
            jax.ShapeDtypeStruct(recv.shape, BF16),
            jax.ShapeDtypeStruct((ranks, hidden + kv), BF16),
            jax.ShapeDtypeStruct((n, ranks), BF16),
            jax.ShapeDtypeStruct((n, ranks), BF16),
        ),
        in_specs=[
            smem,
            smem,
            pl.BlockSpec((1, n), lambda j: (0, 0)),
            pl.BlockSpec(block, lambda j: (0, jnp.minimum(j, last - 1), 0, 0)),
            pl.BlockSpec(block, lambda j: (0, last, 0, 0)),
            pl.BlockSpec((n, width), lambda j: (0, jnp.minimum(j, last))),
            pl.BlockSpec((n, kv), lambda j: (0, 0)),
        ],
        out_specs=(
            pl.BlockSpec(block, lambda j: (0, jnp.maximum(j - 1, 0), 0, 0)),
            pl.BlockSpec(memory_space=pl.ANY),
            pl.BlockSpec((n, ranks), lambda j: (0, 0)),
            pl.BlockSpec((n, ranks), lambda j: (0, 0)),
        ),
        scratch_shapes=[
            pltpu.VMEM((ranks, hidden + kv), BF16),
            pltpu.VMEM((ranks, n), F32),
            pltpu.VMEM((ranks, n), BF16),
            pltpu.VMEM((ranks, n), F32),
            pltpu.VMEM((ranks, hidden + kv), F32),
            pltpu.SemaphoreType.DMA((steps,)),
        ],
        compiler_params=pltpu.CompilerParams(vmem_limit_bytes=56 * MIB),
        cost_estimate=pl.CostEstimate(flops=2**32, bytes_accessed=16 * 2**20, transcendentals=0),
        name="lora",
    )(pos, read, rows, recv, recv, tokens, cotangent)


def adam_kernel(pos_ref, home_ref, read_ref, recv_ref, a_ref, m_ref, v_ref,
                send_ref, new_a_ref, new_m_ref, new_v_ref, acc, packed):
    step = pl.program_id(0)
    tenant, odd = pos_ref[0], (pos_ref[1] & 1) == 1
    devices = recv_ref.shape[0]
    here = a_ref.shape[0]

    @pl.when(step == 0)
    def _():
        acc[...] = jnp.zeros_like(acc)

        def add(d, _):
            acc[slot_of(home_ref, read_ref, d, tenant)] += recv_ref[d].astype(F32)
            return 0

        lax.fori_loop(0, devices, add, 0, unroll=8)

    for i in range(here):
        h = step * here + i
        g = unpack_slice(acc[h], odd)
        m, v, a = (load_tiles(r, i) for r in (m_ref, v_ref, a_ref))
        m = [beta_first * m[j] + (1.0 - beta_first) * g[j] for j in range(5)]
        v = [beta_second * v[j] + (1.0 - beta_second) * g[j] * g[j] for j in range(5)]
        a = [
            a[j]
            - learn_rate * (m[j] / corr_first) / (jnp.sqrt(v[j] / corr_second) + adam_eps)
            for j in range(5)
        ]
        store_tiles(new_m_ref, i, m)
        store_tiles(new_v_ref, i, v)
        store_tiles(new_a_ref, i, a)
        packed[h] = pack_slice(a, odd).astype(BF16)

    @pl.when(step == pl.num_programs(0) - 1)
    def _():
        def copy(d, _):
            send_ref[d] = packed[slot_of(home_ref, read_ref, d, tenant)]
            return 0

        lax.fori_loop(0, devices, copy, 0, unroll=8)


def adam(pos, home, read, recv, adapters, first, second):
    slots = adapters.shape[0]
    steps = 4
    smem = pl.BlockSpec(memory_space=pltpu.SMEM)
    whole = pl.BlockSpec(recv.shape, lambda i: (0, 0, 0))
    part = pl.BlockSpec((slots // steps,) + adapters.shape[1:], lambda i: (i, 0, 0))
    stored = jax.ShapeDtypeStruct(adapters.shape, F32)
    return pl.pallas_call(
        adam_kernel,
        grid=(steps,),
        out_shape=(jax.ShapeDtypeStruct(recv.shape, BF16), stored, stored, stored),
        in_specs=[smem, smem, smem, whole, part, part, part],
        out_specs=(whole, part, part, part),
        scratch_shapes=[
            pltpu.VMEM((slots, PACK, 128), F32),
            pltpu.VMEM((slots, PACK, 128), BF16),
        ],
        compiler_params=pltpu.CompilerParams(vmem_limit_bytes=56 * MIB),
        cost_estimate=pl.CostEstimate(flops=2**24, bytes_accessed=20 * 2**20, transcendentals=0),
        name="adam",
    )(pos, home, read, recv, adapters, first, second)


def refresh_kernel(recv_ref, out_ref):
    for k in range(recv_ref.shape[0]):
        for p in range(recv_ref.shape[1] // 2):
            even, odd = recv_ref[k, 2 * p], recv_ref[k, 2 * p + 1]
            tiles = [even[16 * t : 16 * t + 16] for t in range(4)]
            tiles += [middle_tile(even, odd)]
            tiles += [odd[16 * t : 16 * t + 16] for t in range(4)]
            for t in range(9):
                out_ref[k, :, PAIR * p + 128 * t : PAIR * p + 128 * t + 128] = tiles[t]


def refresh(recv, reads):
    shards = recv.shape[0] // reads
    recv = recv.reshape(reads, shards, PACK, 128)
    return pl.pallas_call(
        refresh_kernel,
        grid=(reads // 4,),
        out_shape=jax.ShapeDtypeStruct((reads, RANK, shards * SECTION), BF16),
        in_specs=[pl.BlockSpec((4, shards, PACK, 128), lambda k: (k, 0, 0, 0))],
        out_specs=pl.BlockSpec((4, RANK, shards * SECTION), lambda k: (k, 0, 0)),
        compiler_params=pltpu.CompilerParams(vmem_limit_bytes=16 * MIB),
        cost_estimate=pl.CostEstimate(flops=0, bytes_accessed=5 * 2**20, transcendentals=0),
        name="refresh",
    )(recv)


def base_kernel(scale, w_hbm, tok_ref, cot_ref, down_ref, up_ref, low_ref, lg_ref,
                values_ref, tg_ref, w, acc, sems):
    i = pl.program_id(0)
    steps = pl.num_programs(0)
    rows = w.shape[1]
    piece = w_hbm.shape[2]
    slot = lax.rem(i, 2)

    def loads(step, at):
        for t in range(rows // piece):
            yield pltpu.make_async_copy(
                w_hbm.at[t % 2, step * (rows // piece // 2) + t // 2],
                w.at[at, pl.ds(piece * t, piece)],
                sems.at[at, t],
            )

    @pl.when(i == 0)
    def _():
        for load in loads(0, 0):
            load.start()
        acc[...] = scale * jnp.dot(low_ref[...], up_ref[...], preferred_element_type=F32)

    @pl.when(i + 1 < steps)
    def _():
        for load in loads(i + 1, 1 - slot):
            load.start()

    for load in loads(i, slot):
        load.wait()
    acc[...] += jnp.dot(tok_ref[...], w[slot], preferred_element_type=F32)
    tg_ref[...] = (
        lax.dot_general(cot_ref[...], w[slot], NT, preferred_element_type=F32)
        + jnp.dot(lg_ref[...], down_ref[...], preferred_element_type=F32)
    ).astype(BF16)

    @pl.when(i == steps - 1)
    def _():
        values_ref[...] = acc[...].astype(BF16)


def base(scale, weight, tokens, cotangent, down, low, lg):
    n, hidden = tokens.shape
    kv = cotangent.shape[1]
    ranks = low.shape[1]
    rows = BASE_ROWS
    piece = weight.shape[2]
    whole = lambda i: (0, 0)
    return pl.pallas_call(
        functools.partial(base_kernel, scale),
        grid=(hidden // rows,),
        out_shape=(
            jax.ShapeDtypeStruct((n, kv), BF16),
            jax.ShapeDtypeStruct((n, hidden), BF16),
        ),
        in_specs=[
            pl.BlockSpec(memory_space=pl.ANY),
            pl.BlockSpec((n, rows), lambda i: (0, i)),
            pl.BlockSpec((n, kv), whole),
            pl.BlockSpec((ranks, rows), lambda i: (0, i)),
            pl.BlockSpec((ranks, kv), lambda i: (0, hidden // kv)),
            pl.BlockSpec((n, ranks), whole),
            pl.BlockSpec((n, ranks), whole),
        ],
        out_specs=(pl.BlockSpec((n, kv), whole), pl.BlockSpec((n, rows), lambda i: (0, i))),
        scratch_shapes=[
            pltpu.VMEM((2, rows, kv), BF16),
            pltpu.VMEM((n, kv), F32),
            pltpu.SemaphoreType.DMA((2, rows // piece)),
        ],
        compiler_params=pltpu.CompilerParams(vmem_limit_bytes=56 * MIB),
        cost_estimate=pl.CostEstimate(flops=18 * 2**30, bytes_accessed=38 * MIB, transcendentals=0),
        name="base",
    )(weight, tokens, cotangent, down, down, low, lg)


def exchange(blocks):
    return lax.all_to_all(blocks, ("x", "core", "y", "z"), split_axis=0, concat_axis=0, tiled=True)


def per_device(
    tokens,
    cotangent,
    value_weight,
    adapters,
    first_moment,
    second_moment,
    tenant_home,
    read_tenants,
    row_tenant,
):
    hidden = tokens.shape[1]
    read_tenants = read_tenants.T
    reads = read_tenants.shape[0]
    core = lax.axis_index("core").astype(jnp.int32)
    shard = lax.axis_index(("y", "z")).astype(jnp.int32)
    pos = jnp.stack([2 * lax.axis_index("x").astype(jnp.int32) + core, shard])
    scale = 2.0 / math.sqrt(hidden * RANK)

    shards = hidden // value_weight.shape[0]
    half = value_weight.shape[0] // 2
    mine = lax.dynamic_slice_in_dim(value_weight, core * half, half, 0)
    weight = lax.all_gather(mine, ("core", "y", "z"), axis=0, tiled=True)
    weight = weight.reshape(2, shards, half, value_weight.shape[1])

    fetched = exchange(pick(pos, tenant_home, read_tenants, adapters))
    send, down, low, lg = lora(
        scale, pos, read_tenants, row_tenant.reshape(1, -1), fetched, tokens, cotangent
    )
    received = exchange(send.reshape(fetched.shape))
    fresh, new_adapters, new_first, new_second = adam(
        pos, tenant_home, read_tenants, received, adapters, first_moment, second_moment
    )
    renewed = exchange(fresh)
    weight, _ = lax.optimization_barrier((weight, fresh))
    values, token_grad = base(scale, weight, tokens, cotangent, down, low, lg)
    values, renewed = lax.optimization_barrier((values, renewed))
    refreshed = refresh(renewed, reads)
    return (values, token_grad, new_adapters, new_first, new_second, refreshed)


def solution(mesh):
    shape = mesh.devices.shape
    inner = Mesh(mesh.devices.reshape(shape[0] // 2, 2, 4, 4), ("x", "core", "y", "z"))
    rows = ("x", "core", "y", "z")
    tenant, fsdp = ("x", "core"), ("y", "z")
    return jax.shard_map(
        per_device,
        mesh=inner,
        in_specs=(
            P(rows, None),
            P(rows, None),
            P(fsdp, None),
            P(tenant, None, fsdp),
            P(tenant, None, fsdp),
            P(tenant, None, fsdp),
            P(),
            P(),
            P(rows),
        ),
        out_specs=(
            P(rows, None),
            P(rows, None),
            P(tenant, None, fsdp),
            P(tenant, None, fsdp),
            P(tenant, None, fsdp),
            P(rows, None, None),
        ),
        check_vma=False,
    )
```

```python
import functools
import math

import jax
import jax.numpy as jnp
from jax import lax
from jax.experimental import pallas as pl
from jax.experimental.pallas import tpu as pltpu
from jax.sharding import Mesh, PartitionSpec as P

beta_first = 0.9
beta_second = 0.95
learn_rate = 0.1
adam_eps = 1e-08
corr_first = 1.0 - 0.9**10
corr_second = 1.0 - 0.95**10

BF16 = jnp.bfloat16
F32 = jnp.float32
NT = (((1,), (1,)), ((), ()))
NN = (((1,), (0,)), ((), ()))
TN = (((0,), (0,)), ((), ()))
MIB = 2**20
BASE_ROWS = 1024
RANK = 16
SECTION = 576
PACK = 72
PAIR = 2 * SECTION
LORA_STEPS = 8


def lane_below(half):
    return lax.broadcasted_iota(jnp.int32, (8, 128), 1) < half


def halves(low, high):
    return jnp.where(lax.broadcasted_iota(jnp.int32, low.shape, 1) < 64, low, high)


def pack_slice(tiles, odd):
    rolled = [pltpu.roll(t, 64, 1) for t in tiles]
    body = [jnp.where(odd, halves(rolled[j], rolled[j + 1]), tiles[j]) for j in range(4)]
    tail = jnp.where(
        odd,
        halves(tiles[0][8:16], rolled[0][0:8]),
        halves(tiles[4][0:8], rolled[4][8:16]),
    )
    return jnp.concatenate(body + [tail], axis=0)


def unpack_slice(block, odd):
    tail = block[64:72]
    tail_rolled = pltpu.roll(tail, 64, 1)
    tiles = [block[16 * j : 16 * j + 16] for j in range(4)]
    rolled = [pltpu.roll(t, 64, 1) for t in tiles]
    last = jnp.concatenate([tail, tail_rolled], axis=0)
    before = jnp.concatenate([tail_rolled, tail], axis=0)
    row = [jnp.where(odd, halves(before, rolled[0]), tiles[0])]
    row += [jnp.where(odd, halves(rolled[j - 1], rolled[j]), tiles[j]) for j in range(1, 4)]
    return row + [jnp.where(odd, rolled[3], last)]


def load_tiles(ref, h):
    tail = jnp.concatenate([ref[h, :, 512:SECTION], jnp.zeros((RANK, 640 - SECTION), F32)], axis=1)
    return [ref[h, :, 128 * j : 128 * j + 128] for j in range(4)] + [tail]


def store_tiles(ref, h, tiles):
    for j in range(4):
        ref[h, :, 128 * j : 128 * j + 128] = tiles[j]
    ref[h, :, 512:SECTION] = tiles[4][:, : SECTION - 512]


def middle_tile(even, odd):
    te, to = even.astype(F32)[64:72], odd.astype(F32)[64:72]
    below = lane_below(64)
    low = jnp.where(below, te, to)
    high = pltpu.roll(jnp.where(below, to, te), 64, 1)
    return jnp.concatenate([low, high], axis=0).astype(BF16)


def slot_of(home_ref, read_ref, d, tenant):
    return home_ref[read_ref[tenant, d]] - RANK * tenant


def pick_kernel(pos_ref, home_ref, read_ref, adapters_ref, out_ref, packed):
    step = pl.program_id(0)
    tenant, odd = pos_ref[0], (pos_ref[1] & 1) == 1
    slots, here = adapters_ref.shape[0], out_ref.shape[0]

    @pl.when(step == 0)
    def _():
        def fill(h, _):
            packed[h] = pack_slice(load_tiles(adapters_ref, h), odd).astype(BF16)
            return 0

        lax.fori_loop(0, slots, fill, 0, unroll=2)

    def copy(d, _):
        out_ref[d] = packed[slot_of(home_ref, read_ref, step * here + d, tenant)]
        return 0

    lax.fori_loop(0, here, copy, 0, unroll=8)


def pick(pos, home, read, adapters):
    slots, devices = adapters.shape[0], read.shape[1]
    steps = 2
    return pl.pallas_call(
        pick_kernel,
        grid=(steps,),
        out_shape=jax.ShapeDtypeStruct((devices, PACK, 128), BF16),
        in_specs=[pl.BlockSpec(memory_space=pltpu.SMEM)] * 3
        + [pl.BlockSpec(adapters.shape, lambda i: (0, 0, 0))],
        out_specs=pl.BlockSpec((devices // steps, PACK, 128), lambda i: (i, 0, 0)),
        scratch_shapes=[pltpu.VMEM((slots, PACK, 128), BF16)],
        compiler_params=pltpu.CompilerParams(vmem_limit_bytes=56 * MIB),
        cost_estimate=pl.CostEstimate(flops=0, bytes_accessed=6 * 2**20, transcendentals=0),
        name="pick",
    )(pos, home, read, adapters)


def lora_kernel(scale, pos_ref, read_ref, rows_ref, recv_ref, last_ref, tok_ref, cot_ref,
                send_ref, down_ref, low_ref, lg_ref, adapter, mask, lgt, low_acc, grad, sems):
    j = pl.program_id(0)
    steps = pl.num_programs(0) - 1
    width = tok_ref.shape[1]
    reads = read_ref.shape[0]
    pairs = recv_ref.shape[1] // 2
    part = pairs * PAIR
    hidden = steps * width

    def assemble(block_ref, p):
        for q in range(pairs):
            base = pl.multiple_of(p * part + q * PAIR, 128)
            for k in range(reads):
                even, odd = block_ref[k, 2 * q], block_ref[k, 2 * q + 1]
                tiles = [even[16 * t : 16 * t + 16] for t in range(4)]
                tiles += [middle_tile(even, odd)]
                tiles += [odd[16 * t : 16 * t + 16] for t in range(4)]
                for t in range(9):
                    adapter[RANK * k : RANK * k + RANK, pl.ds(base + 128 * t, 128)] = tiles[t]

    def keep(p):
        at = pl.ds(pl.multiple_of(p * part, 128), part)
        return pltpu.make_async_copy(adapter.at[:, at], down_ref.at[:, at], sems.at[p])

    @pl.when(j == 0)
    def _():
        assemble(last_ref, steps - 1)
        keep(steps - 1).start()
        device = pos_ref[0] * 16 + pos_ref[1]
        owner = lax.broadcasted_iota(jnp.int32, mask.shape, 0) // RANK
        wanted = jnp.zeros(mask.shape, jnp.int32)
        for k in range(reads):
            wanted = jnp.where(owner == k, read_ref[k, device], wanted)
        mask[...] = (wanted == rows_ref[...]).astype(F32)
        up = adapter[:, hidden:]
        grad_t = scale * lax.dot_general(up, cot_ref[...], NT, preferred_element_type=F32) * mask[...]
        lgt[...] = grad_t.astype(BF16)
        lg_ref[...] = grad_t.T.astype(BF16)
        low_acc[...] = jnp.zeros_like(low_acc)

    @pl.when(j < steps - 1)
    def _():
        assemble(recv_ref, j)
        keep(j).start()

    @pl.when(j < steps)
    def _():
        at = pl.ds(pl.multiple_of(j * width, 128), width)
        low_acc[...] += lax.dot_general(adapter[:, at], tok_ref[...], NT, preferred_element_type=F32)
        grad[:, at] = lax.dot_general(lgt[...], tok_ref[...], NN, preferred_element_type=F32)

    @pl.when(j == steps)
    def _():
        low_t = low_acc[...] * mask[...]
        low_ref[...] = low_t.T.astype(BF16)
        grad[:, hidden:] = scale * lax.dot_general(
            low_t.astype(BF16), cot_ref[...], NN, preferred_element_type=F32
        )

    @pl.when(j > 0)
    def _():
        below = lane_below(64)
        for q in range(pairs):
            base = pl.multiple_of((j - 1) * part + q * PAIR, 128)
            for k in range(reads):
                rows = slice(RANK * k, RANK * k + RANK)
                tiles = [grad[rows, pl.ds(base + 128 * t, 128)] for t in range(9)]
                low, high = tiles[4][0:8], pltpu.roll(tiles[4][8:16], 64, 1)
                first, second = jnp.where(below, low, high), jnp.where(below, high, low)
                send_ref[k, 2 * q] = jnp.concatenate(tiles[:4] + [first], axis=0).astype(BF16)
                send_ref[k, 2 * q + 1] = jnp.concatenate(tiles[5:] + [second], axis=0).astype(BF16)

    @pl.when(j == steps)
    def _():
        for p in range(adapter.shape[1] // part):
            keep(p).wait()


def lora(scale, pos, read, rows, recv, tokens, cotangent):
    n, hidden = tokens.shape
    kv = cotangent.shape[1]
    reads = read.shape[0]
    ranks = reads * RANK
    shards = (hidden + kv) // SECTION
    steps = LORA_STEPS
    width = hidden // steps
    recv = recv.reshape(reads, shards, PACK, 128)
    block = (reads, shards // steps, PACK, 128)
    last = steps - 1
    smem = pl.BlockSpec(memory_space=pltpu.SMEM)
    return pl.pallas_call(
        functools.partial(lora_kernel, scale),
        grid=(steps + 1,),
        out_shape=(
            jax.ShapeDtypeStruct(recv.shape, BF16),
            jax.ShapeDtypeStruct((ranks, hidden + kv), BF16),
            jax.ShapeDtypeStruct((n, ranks), BF16),
            jax.ShapeDtypeStruct((n, ranks), BF16),
        ),
        in_specs=[
            smem,
            smem,
            pl.BlockSpec((1, n), lambda j: (0, 0)),
            pl.BlockSpec(block, lambda j: (0, jnp.minimum(j, last - 1), 0, 0)),
            pl.BlockSpec(block, lambda j: (0, last, 0, 0)),
            pl.BlockSpec((n, width), lambda j: (0, jnp.minimum(j, last))),
            pl.BlockSpec((n, kv), lambda j: (0, 0)),
        ],
        out_specs=(
            pl.BlockSpec(block, lambda j: (0, jnp.maximum(j - 1, 0), 0, 0)),
            pl.BlockSpec(memory_space=pl.ANY),
            pl.BlockSpec((n, ranks), lambda j: (0, 0)),
            pl.BlockSpec((n, ranks), lambda j: (0, 0)),
        ),
        scratch_shapes=[
            pltpu.VMEM((ranks, hidden + kv), BF16),
            pltpu.VMEM((ranks, n), F32),
            pltpu.VMEM((ranks, n), BF16),
            pltpu.VMEM((ranks, n), F32),
            pltpu.VMEM((ranks, hidden + kv), F32),
            pltpu.SemaphoreType.DMA((steps,)),
        ],
        compiler_params=pltpu.CompilerParams(vmem_limit_bytes=56 * MIB),
        cost_estimate=pl.CostEstimate(flops=2**32, bytes_accessed=16 * 2**20, transcendentals=0),
        name="lora",
    )(pos, read, rows, recv, recv, tokens, cotangent)


def adam_kernel(pos_ref, home_ref, read_ref, recv_ref, a_ref, m_ref, v_ref,
                send_ref, new_a_ref, new_m_ref, new_v_ref, acc, packed):
    step = pl.program_id(0)
    tenant, odd = pos_ref[0], (pos_ref[1] & 1) == 1
    devices = recv_ref.shape[0]
    here = a_ref.shape[0]

    @pl.when(step == 0)
    def _():
        acc[...] = jnp.zeros_like(acc)

        def add(d, _):
            acc[slot_of(home_ref, read_ref, d, tenant)] += recv_ref[d].astype(F32)
            return 0

        lax.fori_loop(0, devices, add, 0, unroll=8)

    for i in range(here):
        h = step * here + i
        g = unpack_slice(acc[h], odd)
        m, v, a = (load_tiles(r, i) for r in (m_ref, v_ref, a_ref))
        m = [beta_first * m[j] + (1.0 - beta_first) * g[j] for j in range(5)]
        v = [beta_second * v[j] + (1.0 - beta_second) * g[j] * g[j] for j in range(5)]
        a = [
            a[j]
            - learn_rate * (m[j] / corr_first) / (jnp.sqrt(v[j] / corr_second) + adam_eps)
            for j in range(5)
        ]
        store_tiles(new_m_ref, i, m)
        store_tiles(new_v_ref, i, v)
        store_tiles(new_a_ref, i, a)
        packed[h] = pack_slice(a, odd).astype(BF16)

    @pl.when(step == pl.num_programs(0) - 1)
    def _():
        def copy(d, _):
            send_ref[d] = packed[slot_of(home_ref, read_ref, d, tenant)]
            return 0

        lax.fori_loop(0, devices, copy, 0, unroll=8)


def adam(pos, home, read, recv, adapters, first, second):
    slots = adapters.shape[0]
    steps = 4
    smem = pl.BlockSpec(memory_space=pltpu.SMEM)
    whole = pl.BlockSpec(recv.shape, lambda i: (0, 0, 0))
    part = pl.BlockSpec((slots // steps,) + adapters.shape[1:], lambda i: (i, 0, 0))
    stored = jax.ShapeDtypeStruct(adapters.shape, F32)
    return pl.pallas_call(
        adam_kernel,
        grid=(steps,),
        out_shape=(jax.ShapeDtypeStruct(recv.shape, BF16), stored, stored, stored),
        in_specs=[smem, smem, smem, whole, part, part, part],
        out_specs=(whole, part, part, part),
        scratch_shapes=[
            pltpu.VMEM((slots, PACK, 128), F32),
            pltpu.VMEM((slots, PACK, 128), BF16),
        ],
        compiler_params=pltpu.CompilerParams(vmem_limit_bytes=56 * MIB),
        cost_estimate=pl.CostEstimate(flops=2**24, bytes_accessed=20 * 2**20, transcendentals=0),
        name="adam",
    )(pos, home, read, recv, adapters, first, second)


def refresh_kernel(recv_ref, out_ref):
    for k in range(recv_ref.shape[0]):
        for p in range(recv_ref.shape[1] // 2):
            even, odd = recv_ref[k, 2 * p], recv_ref[k, 2 * p + 1]
            tiles = [even[16 * t : 16 * t + 16] for t in range(4)]
            tiles += [middle_tile(even, odd)]
            tiles += [odd[16 * t : 16 * t + 16] for t in range(4)]
            for t in range(9):
                out_ref[k, :, PAIR * p + 128 * t : PAIR * p + 128 * t + 128] = tiles[t]


def refresh(recv, reads):
    shards = recv.shape[0] // reads
    recv = recv.reshape(reads, shards, PACK, 128)
    return pl.pallas_call(
        refresh_kernel,
        grid=(reads // 2,),
        out_shape=jax.ShapeDtypeStruct((reads, RANK, shards * SECTION), BF16),
        in_specs=[pl.BlockSpec((2, shards, PACK, 128), lambda k: (k, 0, 0, 0))],
        out_specs=pl.BlockSpec((2, RANK, shards * SECTION), lambda k: (k, 0, 0)),
        compiler_params=pltpu.CompilerParams(vmem_limit_bytes=16 * MIB),
        cost_estimate=pl.CostEstimate(flops=0, bytes_accessed=5 * 2**20, transcendentals=0),
        name="refresh",
    )(recv)


def base_kernel(scale, w_hbm, tok_ref, cot_ref, down_ref, up_ref, low_ref, lg_ref,
                values_ref, tg_ref, w, acc, sems):
    i = pl.program_id(0)
    steps = pl.num_programs(0)
    rows = w.shape[1]
    piece = w_hbm.shape[2]
    slot = lax.rem(i, 2)

    def loads(step, at):
        for t in range(rows // piece):
            yield pltpu.make_async_copy(
                w_hbm.at[t % 2, step * (rows // piece // 2) + t // 2],
                w.at[at, pl.ds(piece * t, piece)],
                sems.at[at, t],
            )

    @pl.when(i == 0)
    def _():
        for load in loads(0, 0):
            load.start()
        acc[...] = scale * jnp.dot(low_ref[...], up_ref[...], preferred_element_type=F32)

    @pl.when(i + 1 < steps)
    def _():
        for load in loads(i + 1, 1 - slot):
            load.start()

    for load in loads(i, slot):
        load.wait()
    acc[...] += jnp.dot(tok_ref[...], w[slot], preferred_element_type=F32)
    tg_ref[...] = (
        lax.dot_general(cot_ref[...], w[slot], NT, preferred_element_type=F32)
        + jnp.dot(lg_ref[...], down_ref[...], preferred_element_type=F32)
    ).astype(BF16)

    @pl.when(i == steps - 1)
    def _():
        values_ref[...] = acc[...].astype(BF16)


def base(scale, weight, tokens, cotangent, down, low, lg):
    n, hidden = tokens.shape
    kv = cotangent.shape[1]
    ranks = low.shape[1]
    rows = BASE_ROWS
    piece = weight.shape[2]
    whole = lambda i: (0, 0)
    return pl.pallas_call(
        functools.partial(base_kernel, scale),
        grid=(hidden // rows,),
        out_shape=(
            jax.ShapeDtypeStruct((n, kv), BF16),
            jax.ShapeDtypeStruct((n, hidden), BF16),
        ),
        in_specs=[
            pl.BlockSpec(memory_space=pl.ANY),
            pl.BlockSpec((n, rows), lambda i: (0, i)),
            pl.BlockSpec((n, kv), whole),
            pl.BlockSpec((ranks, rows), lambda i: (0, i)),
            pl.BlockSpec((ranks, kv), lambda i: (0, hidden // kv)),
            pl.BlockSpec((n, ranks), whole),
            pl.BlockSpec((n, ranks), whole),
        ],
        out_specs=(pl.BlockSpec((n, kv), whole), pl.BlockSpec((n, rows), lambda i: (0, i))),
        scratch_shapes=[
            pltpu.VMEM((2, rows, kv), BF16),
            pltpu.VMEM((n, kv), F32),
            pltpu.SemaphoreType.DMA((2, rows // piece)),
        ],
        compiler_params=pltpu.CompilerParams(vmem_limit_bytes=56 * MIB),
        cost_estimate=pl.CostEstimate(flops=18 * 2**30, bytes_accessed=38 * MIB, transcendentals=0),
        name="base",
    )(weight, tokens, cotangent, down, down, low, lg)


def exchange(blocks):
    return lax.all_to_all(blocks, ("x", "core", "y", "z"), split_axis=0, concat_axis=0, tiled=True)


def per_device(
    tokens,
    cotangent,
    value_weight,
    adapters,
    first_moment,
    second_moment,
    tenant_home,
    read_tenants,
    row_tenant,
):
    hidden = tokens.shape[1]
    read_tenants = read_tenants.T
    reads = read_tenants.shape[0]
    core = lax.axis_index("core").astype(jnp.int32)
    shard = lax.axis_index(("y", "z")).astype(jnp.int32)
    pos = jnp.stack([2 * lax.axis_index("x").astype(jnp.int32) + core, shard])
    scale = 2.0 / math.sqrt(hidden * RANK)

    shards = hidden // value_weight.shape[0]
    half = value_weight.shape[0] // 2
    mine = lax.dynamic_slice_in_dim(value_weight, core * half, half, 0)
    weight = lax.all_gather(mine, ("core", "y", "z"), axis=0, tiled=True)
    weight = weight.reshape(2, shards, half, value_weight.shape[1])

    fetched = exchange(pick(pos, tenant_home, read_tenants, adapters))
    send, down, low, lg = lora(
        scale, pos, read_tenants, row_tenant.reshape(1, -1), fetched, tokens, cotangent
    )
    received = exchange(send.reshape(fetched.shape))
    fresh, new_adapters, new_first, new_second = adam(
        pos, tenant_home, read_tenants, received, adapters, first_moment, second_moment
    )
    renewed = exchange(fresh)
    weight, _ = lax.optimization_barrier((weight, fresh))
    values, token_grad = base(scale, weight, tokens, cotangent, down, low, lg)
    values, renewed = lax.optimization_barrier((values, renewed))
    refreshed = refresh(renewed, reads)
    return (values, token_grad, new_adapters, new_first, new_second, refreshed)


def solution(mesh):
    shape = mesh.devices.shape
    inner = Mesh(mesh.devices.reshape(shape[0] // 2, 2, 4, 4), ("x", "core", "y", "z"))
    rows = ("x", "core", "y", "z")
    tenant, fsdp = ("x", "core"), ("y", "z")
    return jax.shard_map(
        per_device,
        mesh=inner,
        in_specs=(
            P(rows, None),
            P(rows, None),
            P(fsdp, None),
            P(tenant, None, fsdp),
            P(tenant, None, fsdp),
            P(tenant, None, fsdp),
            P(),
            P(),
            P(rows),
        ),
        out_specs=(
            P(rows, None),
            P(rows, None),
            P(tenant, None, fsdp),
            P(tenant, None, fsdp),
            P(tenant, None, fsdp),
            P(rows, None, None),
        ),
        check_vma=False,
    )
```
